256 devices in a mesh: lon: 32 (over x_lo, z, core), head: 4 (over y), cfg: 2 (over x_hi).
Axes of the slice: x: 4 (x_hi: 2, x_lo: 2; x = x_hi * 2 + x_lo), y: 4, z: 8, core: 2. Of those that a mesh axis runs over, the one named last changes fastest.
Arguments:
- latents: bfloat16 [2, 2, 48, 192, 1536], P('cfg', None, None, 'lon', 'head'), may hold values from -14 to 14
- timestep: int32 [1], replicated, may hold values from 0 to 999
- guide_num: int32 [1], replicated, may hold values from 20 to 80
- guide_den: int32 [1], replicated, may hold values from 10 to 20
- depth_level: int32 [2, 48, 192], P(None, None, 'lon'), may hold values from 0 to 15
- depth_table: bfloat16 [16, 1536], replicated, may hold values from -6 to 6
- time_weight: bfloat16 [256, 3072], replicated, may hold values from -0.375 to 0.375
- base_q: bfloat16 [1536, 1536], P(None, 'head'), may hold values from -1 to 1
- base_k: bfloat16 [1536, 1536], P(None, 'head'), may hold values from -1 to 1
- base_v: bfloat16 [1536, 1536], P(None, 'head'), may hold values from -0.15625 to 0.15625
- base_o: bfloat16 [1536, 1536], P('head'), may hold values from -0.15625 to 0.15625
- ctrl_q: bfloat16 [1536, 1536], P(None, 'head'), may hold values from -1 to 1
- ctrl_k: bfloat16 [1536, 1536], P(None, 'head'), may hold values from -1 to 1
- ctrl_v: bfloat16 [1536, 1536], P(None, 'head'), may hold values from -0.15625 to 0.15625
- ctrl_o: bfloat16 [1536, 1536], P('head'), may hold values from -0.15625 to 0.15625
- zero_linear: bfloat16 [1536, 1536], P('head'), may hold values from -0.15625 to 0.15625
Outputs:
- guided: bfloat16 [2, 48, 192, 1536], P(None, None, 'lon', ('head', 'cfg'))
The draws below stay inside these ranges and needn't reach their ends.
All inputs are finite; a program needn't handle non-finite values.
Results may differ from the reference program's by a relative error of at most 0.022.
Values may be sent and summed in bfloat16 or wider, within the bound.
A program may use at most 128 MiB of HBM per device.

```python
import math
import jax
import jax.numpy as jnp
from jax import lax

FRAMES = 2
LAT = 48
COLS = 6
HEADS = 24
HD = 64
FREQ = 256
LEVELS = 16
D = 1536
LON = 192
N_LON = 32


def drawn_weight(key):
    random_part = jnp.clip(jax.random.normal(key, (D, D), jnp.float32), -6.0, 6.0) * D ** (-0.5)
    planted = random_part
    return jnp.clip(planted, -1.0, 1.0).astype(jnp.bfloat16)


def drawn_tokens(key):
    subkeys = jax.random.split(key, 1)
    full_shape = (2, FRAMES, LAT, LON, D)
    jitter = jnp.clip(jax.random.normal(subkeys[0], full_shape, jnp.float32), -6.0, 6.0)
    tokens = jitter
    return tokens.astype(jnp.bfloat16)


def draw_latents(key, part):
    key = jax.random.fold_in(key, 3)
    return drawn_tokens(key)


def draw_base_q(key, part):
    key = jax.random.fold_in(key, 11)
    return drawn_weight(key)


def draw_base_k(key, part):
    key = jax.random.fold_in(key, 12)
    return drawn_weight(key)


def draw_ctrl_q(key, part):
    key = jax.random.fold_in(key, 13)
    return drawn_weight(key)


def draw_ctrl_k(key, part):
    key = jax.random.fold_in(key, 14)
    return drawn_weight(key)


def with_ends(values, key, low, largest):
    index_at = [jax.random.randint(jax.random.fold_in(key, axis), (), 0, length) for axis, length in enumerate(values.shape)]
    longest = values.shape.index(max(values.shape))
    beside = index_at[:longest] + [(index_at[longest] + 1) % values.shape[longest]] + index_at[longest + 1:]
    return values.at[tuple(index_at)].set(low).at[tuple(beside)].set(largest)


def shard_levels(key, dims, cuts, least, high):
    loudness = 1.0
    for dim, parts in cuts:
        heights = jax.random.uniform(jax.random.fold_in(jax.random.fold_in(key, 6), dim), (parts,), jnp.float32, least / len(cuts), high / len(cuts))
        loudness = loudness * jnp.repeat(jnp.exp(heights), dims[dim] // parts).reshape((-1,) + (1,) * (len(dims) - 1 - dim))
    return loudness


def centred(stream_key, extent, width, bound, cuts=(), kind=jnp.bfloat16):
    entries = width * jax.random.normal(stream_key, extent, jnp.float32)
    if cuts:
        entries = entries * shard_levels(stream_key, extent, cuts, -0.22, 0.18)
    return jnp.clip(entries, -bound, bound).astype(kind)


def setup_inputs(seed: int = 0) -> dict:
    arg_keys = jax.random.split(jax.random.key(seed), 17)
    return {
        "latents": draw_latents(jax.random.fold_in(arg_keys[16], 71), 0),
        "timestep": jax.random.randint(arg_keys[1], (1,), 0, 1000).astype(jnp.int32),
        "guide_num": jax.random.randint(arg_keys[2], (1,), 20, 81).astype(jnp.int32),
        "guide_den": jax.random.randint(arg_keys[3], (1,), 10, 21).astype(jnp.int32),
        "depth_level": with_ends(jax.random.randint(arg_keys[4], (FRAMES, LAT, LON), 0, LEVELS), jax.random.fold_in(arg_keys[4], 1), 0, LEVELS - 1).astype(jnp.int32),
        "depth_table": centred(arg_keys[5], (LEVELS, D), 1.0, 6.0),
        "time_weight": centred(arg_keys[6], (FREQ, 2 * D), FREQ ** -0.5, 0.375),
        "base_q": draw_base_q(jax.random.fold_in(arg_keys[16], 71), 0),
        "base_k": draw_base_k(jax.random.fold_in(arg_keys[16], 71), 0),
        "base_v": centred(arg_keys[9], (D, D), D ** -0.5, 0.15625, ((1, 4),)),
        "base_o": centred(arg_keys[10], (D, D), D ** -0.5, 0.15625, ((0, 4),)),
        "ctrl_q": draw_ctrl_q(jax.random.fold_in(arg_keys[16], 71), 0),
        "ctrl_k": draw_ctrl_k(jax.random.fold_in(arg_keys[16], 71), 0),
        "ctrl_v": centred(arg_keys[13], (D, D), D ** -0.5, 0.15625, ((1, 4),)),
        "ctrl_o": centred(arg_keys[14], (D, D), D ** -0.5, 0.15625, ((0, 4),)),
        "zero_linear": centred(arg_keys[15], (D, D), D ** -0.5, 0.15625, ((0, 4),)),
    }


def embed_time(timestep, time_weight):
    half_count = FREQ // 2
    freqs = jnp.exp(-math.log(10000.0) * jnp.arange(half_count).astype(jnp.float32) / half_count)
    angles = timestep.astype(jnp.float32)[0] * freqs
    temb = jnp.concatenate([jnp.cos(angles), jnp.sin(angles)]).astype(jnp.bfloat16)
    modulation = jnp.dot(temb[None, :], time_weight, preferred_element_type=jnp.float32)[0]
    return (modulation[:D], modulation[D:])

def modulate(inputs, scale, shift):
    center = lax.optimization_barrier(jnp.mean(inputs, axis=-1, keepdims=True))
    spread = lax.optimization_barrier(jnp.mean((inputs - center) ** 2, axis=-1, keepdims=True))
    normed = (inputs - center) * lax.rsqrt(spread + 1e-06)
    return (normed * (1.0 + scale) + shift).astype(jnp.bfloat16)

def tile_attention(queries, keys, values):
    tok_count = FRAMES * LAT * COLS
    key_pad = jnp.concatenate([keys[:, :, -COLS:], keys, keys[:, :, :COLS]], axis=2)
    val_pad = jnp.concatenate([values[:, :, -COLS:], values, values[:, :, :COLS]], axis=2)
    qcol = jnp.arange(tok_count) % COLS + COLS
    kcol = jnp.arange(3 * tok_count) % (3 * COLS)
    allowed = jnp.abs(kcol[None, :] - qcol[:, None]) <= COLS

    def one_slab(slab):
        start = (slab * COLS).astype(jnp.int32)
        qs = lax.dynamic_slice_in_dim(queries, start, COLS, 2).reshape(tok_count, HEADS, HD)
        ks = lax.dynamic_slice_in_dim(key_pad, start, 3 * COLS, 2).reshape(3 * tok_count, HEADS, HD)
        vs = lax.dynamic_slice_in_dim(val_pad, start, 3 * COLS, 2).reshape(3 * tok_count, HEADS, HD)
        scores = jnp.einsum('qhd,khd->hqk', qs.astype(jnp.float32), ks.astype(jnp.float32)) * (1.0 / math.sqrt(HD))
        scores = jnp.where(allowed[None], scores, -1e+30)
        top = lax.optimization_barrier(jnp.max(scores, axis=-1, keepdims=True))
        expo = jnp.exp(scores - top)
        weights = (expo / lax.optimization_barrier(jnp.sum(expo, axis=-1, keepdims=True))).astype(jnp.bfloat16)
        mixed = jnp.einsum('hqk,khd->qhd', weights.astype(jnp.float32), vs.astype(jnp.float32))
        return mixed.astype(jnp.bfloat16).reshape(FRAMES, LAT, COLS, D)
    slabs = lax.map(one_slab, jnp.arange(N_LON).astype(jnp.int32))
    return slabs.transpose(1, 2, 0, 3, 4).reshape(FRAMES, LAT, LON, D)

def branch(inputs, scale, shift, w_query, w_key, w_value, w_out):
    normed = modulate(inputs, scale, shift)
    queries = jnp.dot(normed, w_query, preferred_element_type=jnp.float32).astype(jnp.bfloat16)
    keys = jnp.dot(normed, w_key, preferred_element_type=jnp.float32).astype(jnp.bfloat16)
    values = jnp.dot(normed, w_value, preferred_element_type=jnp.float32).astype(jnp.bfloat16)
    mixed = tile_attention(queries, keys, values)
    return jnp.dot(mixed, w_out, preferred_element_type=jnp.float32)

def reference(latents, timestep, guide_num, guide_den, depth_level, depth_table, time_weight, base_q, base_k, base_v, base_o, ctrl_q, ctrl_k, ctrl_v, ctrl_o, zero_linear):
    scale, shift = embed_time(timestep, time_weight)
    cond_in = latents[0].astype(jnp.float32)
    uncond_in = latents[1].astype(jnp.float32)
    base_cond = branch(cond_in, scale, shift, base_q, base_k, base_v, base_o)
    base_uncond = branch(uncond_in, scale, shift, base_q, base_k, base_v, base_o)
    onehot = (depth_level[..., None] == jnp.arange(LEVELS).astype(jnp.int32)).astype(jnp.bfloat16)
    depth_emb = jnp.dot(onehot, depth_table, preferred_element_type=jnp.float32)
    ctrl_out = branch(cond_in + depth_emb, scale, shift, ctrl_q, ctrl_k, ctrl_v, ctrl_o).astype(jnp.bfloat16)
    ctrl_res = jnp.dot(ctrl_out, zero_linear, preferred_element_type=jnp.float32)
    y_cond = cond_in + base_cond + ctrl_res
    y_uncond = uncond_in + base_uncond
    ratio = guide_num[0].astype(jnp.float32) / guide_den[0].astype(jnp.float32)
    return (y_uncond + ratio * (y_cond - y_uncond)).astype(jnp.bfloat16)
```

```python
import functools
import math

import jax
import jax.numpy as jnp
from jax import lax
from jax.experimental import pallas as pl
from jax.experimental.pallas import tpu as pltpu
from jax.sharding import PartitionSpec as P

HD = 64
FREQ = 256
PAIR = 2 * HD
GROUP = 2
BASE, CTRL = 0, 1
F32 = jnp.float32
BF16 = jnp.bfloat16
MESH = pl.DeviceIdType.MESH


def embed_time(timestep):
    half_count = FREQ // 2
    freqs = jnp.exp(-math.log(10000.0) * jnp.arange(half_count).astype(F32) / half_count)
    angles = timestep.astype(F32)[0] * freqs
    temb = jnp.concatenate([jnp.cos(angles), jnp.sin(angles)]).astype(BF16)
    return jnp.broadcast_to(temb[None, :], (16, FREQ))


def attend_pair(q, k, v):
    rows = q.shape[0]
    low = lax.broadcasted_iota(jnp.int32, (rows, PAIR), 1) < HD
    zero = jnp.zeros_like(q)
    both = jnp.concatenate([jnp.where(low, q, zero), jnp.where(low, zero, q)], axis=0)
    scores = lax.dot_general(both, k, (((1,), (1,)), ((), ())), preferred_element_type=F32)
    top = jnp.max(scores, axis=1, keepdims=True)
    expo = jnp.exp2(scores - top).astype(BF16)
    ones = jnp.concatenate([v, jnp.ones_like(v)], axis=1)
    mixed = jnp.dot(expo, ones, preferred_element_type=F32)
    mixed = mixed[:, :PAIR] / mixed[:, PAIR:]
    return jnp.where(low, mixed[:rows], mixed[rows:]).astype(BF16)


def kernel(
    dims,
    x_hbm,
    temb_ref,
    ratio_ref,
    onehot_ref,
    table_ref,
    tw_hbm,
    bq_hbm,
    bk_hbm,
    bv_hbm,
    bo_hbm,
    cq_hbm,
    ck_hbm,
    cv_hbm,
    co_hbm,
    zl_hbm,
    out_ref,
    xg,
    tw,
    wqkv,
    wo,
    mod,
    ms,
    q,
    kv,
    att,
    csum,
    part,
    r1,
    r2,
    kept,
    give,
    take,
    load_sem,
    g_send,
    g_recv,
    h_send,
    h_recv,
    s1_send,
    s1_recv,
    s2_send,
    s2_recv,
    c_send,
    c_recv,
):
    frames, rows, cols, feat, n_lon, n_head = dims
    C = frames * rows
    T = C * cols
    width = feat * n_head
    groups = cols // GROUP
    G = GROUP * C
    lon, head, cfg = lax.axis_index("lon"), lax.axis_index("head"), lax.axis_index("cfg")
    is_cond = cfg == 0
    hp, hm, ho = lax.rem(head + 1, n_head), lax.rem(head + n_head - 1, n_head), lax.rem(head + 2, n_head)
    lp, lm = lax.rem(lon + 1, n_lon), lax.rem(lon + n_lon - 1, n_lon)
    to_hp, to_hm = (lon, hp, cfg), (lon, hm, cfg)
    to_lp, to_lm = (lp, head, cfg), (lm, head, cfg)
    to_cfg = (lon, head, 1 - cfg)

    own_copy = pltpu.make_async_copy(x_hbm, xg.at[head], load_sem.at[0])
    own_copy.start()
    loads = [
        (tw_hbm, tw),
        (cq_hbm, wqkv.at[CTRL, :, pl.ds(0, feat)]),
        (ck_hbm, wqkv.at[CTRL, :, pl.ds(feat, feat)]),
        (cv_hbm, wqkv.at[CTRL, :, pl.ds(2 * feat, feat)]),
        (bq_hbm, wqkv.at[BASE, :, pl.ds(0, feat)]),
        (bk_hbm, wqkv.at[BASE, :, pl.ds(feat, feat)]),
        (bv_hbm, wqkv.at[BASE, :, pl.ds(2 * feat, feat)]),
        (co_hbm, wo.at[CTRL]),
        (bo_hbm, wo.at[BASE]),
        (zl_hbm, wo.at[2]),
    ]
    loads = [pltpu.make_async_copy(s, d, load_sem.at[i + 1]) for i, (s, d) in enumerate(loads)]

    barrier = pltpu.get_barrier_semaphore()
    for who in (to_hp, to_hm, to_lp, to_lm, to_cfg):
        pl.semaphore_signal(barrier, inc=1, device_id=who, device_id_type=MESH)
    for copy in loads:
        copy.start()
    pl.semaphore_wait(barrier, 5)
    own_copy.wait()

    def send(src, dst, ssem, rsem, who):
        return pltpu.make_async_remote_copy(
            src_ref=src, dst_ref=dst, send_sem=ssem, recv_sem=rsem, device_id=who, device_id_type=MESH
        )

    def gather(slot, c, kind, who):
        place = xg.at[slot, :, c]
        return send(place, place, g_send.at[kind, c], g_recv.at[kind, c], who)

    def own_sends(c):
        gather(head, c, 0, to_hp).start()
        gather(head, c, 1, to_hm).start()

    def serve(c):
        gather(hm, c, 0, to_hp).wait_recv()
        gather(hp, c, 1, to_hm).wait_recv()
        if c % 2 == 0:
            gather(hm, c, 2, to_hp).start()
        else:
            gather(hp, c, 2, to_hm).start()
        if c + 3 < cols:
            own_sends(c + 3)

    def halo(branch, g, side, row0):
        src = kv.at[branch, pl.ds(T + row0, G)]
        dst = kv.at[branch, pl.ds((0 if side == 0 else 2 * T) + row0, G)]
        who = to_lp if side == 0 else to_lm
        return send(src, dst, h_send.at[branch, g, side], h_recv.at[branch, g, side], who)

    def normalise(branch, c, at):
        parts = [xg[j, :, c].reshape(C, feat).astype(F32) for j in range(n_head)]
        if branch == CTRL:
            hot = onehot_ref[pl.ds(c * C, C), :]
            for j in range(n_head):
                emb = jnp.dot(hot, table_ref[:, j * feat : (j + 1) * feat], preferred_element_type=F32)
                parts[j] = parts[j] + emb
        center = sum(jnp.sum(u, axis=1, keepdims=True) for u in parts) * (1.0 / width)
        parts = [u - center for u in parts]
        spread = sum(jnp.sum(u * u, axis=1, keepdims=True) for u in parts) * (1.0 / width)
        scale = lax.rsqrt(spread + 1e-06)
        for j in range(n_head):
            sl = pl.ds(j * feat, feat)
            gain = 1.0 + mod[0:1, sl]
            shift = mod[0:1, pl.ds(width + j * feat, feat)]
            ms[branch, pl.ds(at, C), sl] = (parts[j] * scale * gain + shift).astype(BF16)

    def project(branch, g):
        for c in range(GROUP):
            normalise(branch, g * GROUP + c, c * C)
        row0 = g * G
        normed = ms[branch]
        query = jnp.dot(normed, wqkv[branch, :, :feat], preferred_element_type=F32)
        q[branch, pl.ds(row0, G), :] = (query * (math.log2(math.e) / math.sqrt(HD))).astype(BF16)
        kv[branch, pl.ds(T + row0, G), :] = jnp.dot(
            normed, wqkv[branch, :, feat:], preferred_element_type=F32
        ).astype(BF16)

    for c in range(3):
        own_sends(c)
    loads[0].wait()
    mod[...] = jnp.dot(temb_ref[...], tw[...], preferred_element_type=F32)
    for copy in loads[1:]:
        copy.wait()

    served = 0
    for g in range(groups):
        until = min(cols, (g + 2) * GROUP)
        for c in range(served, until):
            serve(c)
        served = until
        for c in range(g * GROUP, (g + 1) * GROUP):
            gather(ho, c, 2, to_hp).wait_recv()

        @pl.when(is_cond)
        def _():
            project(CTRL, g)
            for side in range(2):
                halo(CTRL, g, side, g * G).start()

        project(BASE, g)

        @pl.when(jnp.logical_not(is_cond))
        def _():
            for side in range(2):
                halo(BASE, g, side, g * G).start()

    @pl.when(is_cond)
    def _():
        for g in range(groups):
            for side in range(2):
                halo(BASE, g, side, g * G).start()

    half = C // 2

    def stage1(j, way):
        src = part.at[j, ho, pl.ds(way * half, half)]
        return send(src, r1.at[j, way], s1_send.at[j, way], s1_recv.at[j, way], to_hp if way == 0 else to_hm)

    def stage2(j, way):
        src = part.at[j, hp if way == 0 else hm]
        return send(src, r2.at[j, way], s2_send.at[j, way], s2_recv.at[j, way], to_hp if way == 0 else to_hm)

    def swap(c):
        return send(give.at[c], take.at[c], c_send.at[c], c_recv.at[c], to_cfg)

    def finish(c, mine, other):
        ratio = ratio_ref[0]
        cond = jnp.where(is_cond, mine, other)
        uncond = jnp.where(is_cond, other, mine)
        res = (uncond + ratio * (cond - uncond)).astype(BF16)
        out_ref[:, c] = res.reshape(frames, rows, feat // 2)

    first = jnp.where(is_cond, 0, cols)

    def wait_halo(branch, g, side):
        halo(branch, g, side, g * G).wait_recv()

    @pl.loop(first, 2 * cols + 2)
    def _(i):
        @pl.when(i < 2 * cols)
        def _():
            branch = jnp.where(i < cols, CTRL, BASE)
            c = jnp.where(i < cols, i, i - cols)

            @pl.when(c == 0)
            def _():
                for g in range(groups):
                    wait_halo(branch, g, 0)

            @pl.when(lax.rem(c, GROUP) == 0)
            def _():
                wait_halo(branch, lax.div(c, GROUP), 1)

            r0 = pl.multiple_of(c * C, C)
            n_keys = (2 * cols + 1) * C
            for p in range(feat // PAIR):
                sl = pl.ds(p * PAIR, PAIR)
                att[:, sl] = attend_pair(
                    q[branch, pl.ds(r0, C), sl],
                    kv[branch, pl.ds(r0, n_keys), sl],
                    kv[branch, pl.ds(r0, n_keys), pl.ds(feat + p * PAIR, PAIR)],
                )

            with_ctrl = jnp.logical_and(is_cond, i >= cols)

            @pl.when(with_ctrl)
            def _():
                for d in range(n_head):
                    sl = pl.ds(d * feat, feat)
                    both = jnp.dot(att[...], wo[BASE, :, sl], preferred_element_type=F32)
                    both += jnp.dot(csum[c], wo[2, :, sl], preferred_element_type=F32)
                    part[i, d] = both.astype(BF16)

            @pl.when(jnp.logical_not(with_ctrl))
            def _():
                for d in range(n_head):
                    sl = pl.ds(d * feat, feat)
                    part[i, d] = jnp.dot(att[...], wo[branch, :, sl], preferred_element_type=F32).astype(BF16)

            stage1(i, 0).start()
            stage1(i, 1).start()

        j = i - 1

        @pl.when(jnp.logical_and(j >= first, j < 2 * cols))
        def _():
            stage1(j, 0).wait_recv()
            part[j, hp, pl.ds(0, half)] = (part[j, hp, pl.ds(0, half)].astype(F32) + r1[j, 0].astype(F32)).astype(BF16)
            stage2(j, 0).start()
            stage1(j, 1).wait_recv()
            part[j, hm, pl.ds(half, half)] = (
                part[j, hm, pl.ds(half, half)].astype(F32) + r1[j, 1].astype(F32)
            ).astype(BF16)
            stage2(j, 1).start()

        n = i - 2

        @pl.when(n >= first)
        def _():
            stage2(n, 0).wait_recv()
            stage2(n, 1).wait_recv()
            total = part[n, head].astype(F32) + r2[n, 0].astype(F32) + r2[n, 1].astype(F32)

            @pl.when(n < cols)
            def _():
                csum[n] = total.astype(BF16)

            @pl.when(n >= cols)
            def _():
                c = n - cols
                block = xg[head, :, c].reshape(C, feat).astype(F32) + total
                low, high = block[:, : feat // 2], block[:, feat // 2 :]
                give[c] = jnp.where(is_cond, high, low).astype(BF16)
                swap(c).start()
                mine = jnp.where(is_cond, low, high)

                @pl.when(is_cond)
                def _():
                    swap(c).wait_recv()
                    finish(c, mine, take[c].astype(F32))

                @pl.when(jnp.logical_not(is_cond))
                def _():
                    kept[c] = mine

    @pl.when(jnp.logical_not(is_cond))
    def _():
        @pl.loop(0, cols)
        def _(c):
            swap(c).wait_recv()
            finish(c, kept[c], take[c].astype(F32))

    for c in range(cols):
        gather(head, c, 0, to_hp).wait_send()
        gather(head, c, 1, to_hm).wait_send()
        gather(hm, c, 2, to_hp).wait_send()

    for g in range(groups):
        for side in range(2):
            halo(BASE, g, side, g * G).wait_send()

    @pl.when(is_cond)
    def _():
        for g in range(groups):
            for side in range(2):
                halo(CTRL, g, side, g * G).wait_send()

    @pl.loop(first, 2 * cols)
    def _(j):
        for way in range(2):
            stage1(j, way).wait_send()
            stage2(j, way).wait_send()

    @pl.loop(0, cols)
    def _(c):
        swap(c).wait_send()


def local(
    latents,
    timestep,
    guide_num,
    guide_den,
    depth_level,
    depth_table,
    time_weight,
    base_q,
    base_k,
    base_v,
    base_o,
    ctrl_q,
    ctrl_k,
    ctrl_v,
    ctrl_o,
    zero_linear,
):
    x = latents[0].transpose(0, 2, 1, 3)
    frames, cols, rows, feat = x.shape
    n_lon, n_head = lax.axis_size("lon"), lax.axis_size("head")
    C, T, width = frames * rows, frames * rows * cols, feat * n_head
    levels = depth_table.shape[0]
    temb = embed_time(timestep)
    ratio = guide_num.astype(F32) / guide_den.astype(F32)
    onehot = (depth_level.transpose(2, 0, 1).reshape(T, 1) == jnp.arange(levels)).astype(BF16)
    dma = pltpu.SemaphoreType.DMA
    vmem = pl.BlockSpec(memory_space=pltpu.VMEM)
    smem = pl.BlockSpec(memory_space=pltpu.SMEM)
    hbm = pl.BlockSpec(memory_space=pl.ANY)
    groups = cols // GROUP
    out = pl.pallas_call(
        functools.partial(kernel, (frames, rows, cols, feat, n_lon, n_head)),
        out_shape=jax.ShapeDtypeStruct((frames, cols, rows, feat // 2), BF16),
        in_specs=[hbm, vmem, smem, vmem, vmem] + [hbm] * 10,
        out_specs=vmem,
        scratch_shapes=[
            pltpu.VMEM((n_head, frames, cols, rows, feat), BF16),
            pltpu.VMEM((FREQ, 2 * width), BF16),
            pltpu.VMEM((2, width, 3 * feat), BF16),
            pltpu.VMEM((3, feat, width), BF16),
            pltpu.VMEM((16, 2 * width), F32),
            pltpu.VMEM((2, GROUP * C, width), BF16),
            pltpu.VMEM((2, T, feat), BF16),
            pltpu.VMEM((2, 3 * T, 2 * feat), BF16),
            pltpu.VMEM((C, feat), BF16),
            pltpu.VMEM((cols, C, feat), BF16),
            pltpu.VMEM((2 * cols, n_head, C, feat), BF16),
            pltpu.VMEM((2 * cols, 2, C // 2, feat), BF16),
            pltpu.VMEM((2 * cols, 2, C, feat), BF16),
            pltpu.VMEM((cols, C, feat // 2), F32),
            pltpu.VMEM((cols, C, feat // 2), BF16),
            pltpu.VMEM((cols, C, feat // 2), BF16),
            dma((11,)),
            dma((3, cols)),
            dma((3, cols)),
            dma((2, groups, 2)),
            dma((2, groups, 2)),
            dma((2 * cols, 2)),
            dma((2 * cols, 2)),
            dma((2 * cols, 2)),
            dma((2 * cols, 2)),
            dma((cols,)),
            dma((cols,)),
        ],
        compiler_params=pltpu.CompilerParams(
            collective_id=0, has_side_effects=True, vmem_limit_bytes=58 * 1024 * 1024
        ),
    )(
        x,
        temb,
        ratio,
        onehot,
        depth_table,
        time_weight,
        base_q,
        base_k,
        base_v,
        base_o,
        ctrl_q,
        ctrl_k,
        ctrl_v,
        ctrl_o,
        zero_linear,
    )
    return out.transpose(0, 2, 1, 3)


def solution(mesh):
    return jax.shard_map(
        local,
        mesh=mesh,
        in_specs=(
            P("cfg", None, None, "lon", "head"),
            P(),
            P(),
            P(),
            P(None, None, "lon"),
            P(),
            P(),
            P(None, "head"),
            P(None, "head"),
            P(None, "head"),
            P("head", None),
            P(None, "head"),
            P(None, "head"),
            P(None, "head"),
            P("head", None),
            P("head", None),
        ),
        out_specs=P(None, None, "lon", ("head", "cfg")),
        check_vma=False,
    )
```

```python
import functools
import math

import jax
import jax.numpy as jnp
from jax import lax
from jax.experimental import pallas as pl
from jax.experimental.pallas import tpu as pltpu
from jax.sharding import PartitionSpec as P

HD = 64
FREQ = 256
PAIR = 2 * HD
GROUP = 2
BASE, CTRL = 0, 1
F32 = jnp.float32
BF16 = jnp.bfloat16
MESH = pl.DeviceIdType.MESH


def attend_pair(q, k, v):
    rows = q.shape[0]
    low = lax.broadcasted_iota(jnp.int32, (rows, PAIR), 1) < HD
    zero = jnp.zeros_like(q)
    both = jnp.concatenate([jnp.where(low, q, zero), jnp.where(low, zero, q)], axis=0)
    scores = lax.dot_general(both, k, (((1,), (1,)), ((), ())), preferred_element_type=F32)
    top = jnp.max(scores, axis=1, keepdims=True)
    expo = jnp.exp2(scores - top).astype(BF16)
    ones = jnp.concatenate([v, jnp.ones_like(v)], axis=1)
    mixed = jnp.dot(expo, ones, preferred_element_type=F32)
    mixed = mixed[:, :PAIR] / mixed[:, PAIR:]
    return jnp.where(low, mixed[:rows], mixed[rows:]).astype(BF16)


def kernel(
    dims,
    x_hbm,
    step_ref,
    num_ref,
    den_ref,
    level_ref,
    freq_ref,
    table_ref,
    tw_hbm,
    bq_hbm,
    bk_hbm,
    bv_hbm,
    bo_hbm,
    cq_hbm,
    ck_hbm,
    cv_hbm,
    co_hbm,
    zl_hbm,
    out_ref,
    xg,
    tw,
    wqkv,
    wo,
    mod,
    ms,
    q,
    kv,
    att,
    csum,
    part,
    r1,
    r2,
    kept,
    give,
    take,
    load_sem,
    g_send,
    g_recv,
    h_send,
    h_recv,
    s1_send,
    s1_recv,
    s2_send,
    s2_recv,
    f_send,
    f_recv,
):
    frames, rows, cols, feat, n_lon, n_head = dims
    C = frames * rows
    T = C * cols
    width = feat * n_head
    groups = cols // GROUP
    G = GROUP * C
    lon, head, cfg = lax.axis_index("lon"), lax.axis_index("head"), lax.axis_index("cfg")
    is_cond = cfg == 0
    hp, hm, ho = lax.rem(head + 1, n_head), lax.rem(head + n_head - 1, n_head), lax.rem(head + 2, n_head)
    lp, lm = lax.rem(lon + 1, n_lon), lax.rem(lon + n_lon - 1, n_lon)
    to_hp, to_hm = (lon, hp, cfg), (lon, hm, cfg)
    to_lp, to_lm = (lp, head, cfg), (lm, head, cfg)
    half_feat = feat // 2
    heads = [head, hp, ho, hm]

    own_copy = pltpu.make_async_copy(x_hbm, xg.at[head], load_sem.at[0])
    own_copy.start()
    loads = [
        (tw_hbm, tw),
        (cq_hbm, wqkv.at[CTRL, :, pl.ds(0, feat)]),
        (ck_hbm, wqkv.at[CTRL, :, pl.ds(feat, feat)]),
        (cv_hbm, wqkv.at[CTRL, :, pl.ds(2 * feat, feat)]),
        (bq_hbm, wqkv.at[BASE, :, pl.ds(0, feat)]),
        (bk_hbm, wqkv.at[BASE, :, pl.ds(feat, feat)]),
        (bv_hbm, wqkv.at[BASE, :, pl.ds(2 * feat, feat)]),
    ]
    for at, w in ((CTRL, co_hbm), (BASE, bo_hbm), (2, zl_hbm)):
        loads += [(w.at[:, pl.ds(d * feat, feat)], wo.at[at, d]) for d in range(n_head)]
    loads = [pltpu.make_async_copy(s, d, load_sem.at[i + 1]) for i, (s, d) in enumerate(loads)]

    barrier = pltpu.get_barrier_semaphore()
    group = [(lon, h, cfg) for h in heads[1:]] + [(lon, h, 1 - cfg) for h in heads]
    for who in group + [to_lp, to_lm]:
        pl.semaphore_signal(barrier, inc=1, device_id=who, device_id_type=MESH)
    for copy in loads:
        copy.start()
    pl.semaphore_wait(barrier, len(group) + 2)

    def send(src, dst, ssem, rsem, who):
        return pltpu.make_async_remote_copy(
            src_ref=src, dst_ref=dst, send_sem=ssem, recv_sem=rsem, device_id=who, device_id_type=MESH
        )

    def gather(slot, c, kind, who):
        place = xg.at[slot, :, c]
        return send(place, place, g_send.at[kind, c], g_recv.at[kind, c], who)

    def own_send(c, kind, who):
        return send(x_hbm.at[:, c], xg.at[head, :, c], g_send.at[kind, c], g_recv.at[kind, c], who)

    def own_sends(c):
        own_send(c, 0, to_hp).start()
        own_send(c, 1, to_hm).start()

    def serve(c):
        gather(hm, c, 0, to_hp).wait_recv()
        gather(hp, c, 1, to_hm).wait_recv()
        if c % 2 == 0:
            gather(hm, c, 2, to_hp).start()
        else:
            gather(hp, c, 2, to_hm).start()
        if c + 3 < cols:
            own_sends(c + 3)

    def halo(branch, g, side, row0):
        src = kv.at[branch, pl.ds(T + row0, G)]
        dst = kv.at[branch, pl.ds((0 if side == 0 else 2 * T) + row0, G)]
        who = to_lp if side == 0 else to_lm
        return send(src, dst, h_send.at[branch, g, side], h_recv.at[branch, g, side], who)

    def normalise(branch, c, at):
        parts = [xg[j, :, c].reshape(C, feat).astype(F32) for j in range(n_head)]
        if branch == CTRL:
            levels = lax.broadcasted_iota(jnp.int32, (table_ref.shape[0], rows), 0)
            hot = [jnp.where(levels == level_ref[c, f : f + 1, :], 1.0, 0.0).astype(BF16) for f in range(frames)]
            for j in range(n_head):
                table = table_ref[:, j * feat : (j + 1) * feat]
                emb = [
                    lax.dot_general(h, table, (((0,), (0,)), ((), ())), preferred_element_type=F32) for h in hot
                ]
                parts[j] = parts[j] + jnp.concatenate(emb, axis=0)
        center = sum(jnp.sum(u, axis=1, keepdims=True) for u in parts) * (1.0 / width)
        parts = [u - center for u in parts]
        spread = sum(jnp.sum(u * u, axis=1, keepdims=True) for u in parts) * (1.0 / width)
        scale = lax.rsqrt(spread + 1e-06)
        for j in range(n_head):
            sl = pl.ds(j * feat, feat)
            gain = 1.0 + mod[0:1, sl]
            shift = mod[0:1, pl.ds(width + j * feat, feat)]
            ms[branch, pl.ds(at, C), sl] = (parts[j] * scale * gain + shift).astype(BF16)

    def project(branch, g):
        for c in range(GROUP):
            normalise(branch, g * GROUP + c, c * C)
        row0 = g * G
        normed = ms[branch]
        query = jnp.dot(normed, wqkv[branch, :, :feat], preferred_element_type=F32)
        q[branch, pl.ds(row0, G), :] = (query * (math.log2(math.e) / math.sqrt(HD))).astype(BF16)
        kv[branch, pl.ds(T + row0, G), :] = jnp.dot(
            normed, wqkv[branch, :, feat:], preferred_element_type=F32
        ).astype(BF16)

    for c in range(3):
        own_sends(c)

    @pl.when(jnp.logical_not(is_cond))
    def _():
        csum[...] = jnp.zeros_like(csum)

    angles = freq_ref[...] * step_ref[0].astype(F32)
    temb = jnp.concatenate([jnp.cos(angles), jnp.sin(angles)], axis=1).astype(BF16)
    loads[0].wait()
    mod[...] = jnp.dot(temb, tw[...], preferred_element_type=F32)
    ones = jnp.ones((8, feat), F32)
    ratio = (ones * num_ref[0].astype(F32)) / (ones * den_ref[0].astype(F32))
    factor = jnp.where(is_cond, ratio, 1.0 - ratio)[0:1, :]
    own_copy.wait()
    for copy in loads[1:]:
        copy.wait()

    served = 0
    for g in range(groups):
        until = min(cols, (g + 2) * GROUP)
        for c in range(served, until):
            serve(c)
        served = until
        for c in range(g * GROUP, (g + 1) * GROUP):
            gather(ho, c, 2, to_hp).wait_recv()

        @pl.when(is_cond)
        def _():
            project(CTRL, g)
            for side in range(2):
                halo(CTRL, g, side, g * G).start()

        project(BASE, g)

        @pl.when(jnp.logical_not(is_cond))
        def _():
            for side in range(2):
                halo(BASE, g, side, g * G).start()

    @pl.when(is_cond)
    def _():
        for g in range(groups):
            for side in range(2):
                halo(BASE, g, side, g * G).start()

    def stage1(j, way):
        src = part.at[j, ho, pl.ds(way * C, C)]
        return send(src, r1.at[j, way], s1_send.at[j, way], s1_recv.at[j, way], to_hp if way == 0 else to_hm)

    def stage2(j, way):
        src = part.at[j, hp if way == 0 else hm]
        return send(src, r2.at[j, way], s2_send.at[j, way], s2_recv.at[j, way], to_hp if way == 0 else to_hm)

    def relay(j):
        for way, d in ((0, hp), (1, hm)):
            stage1(j, way).wait_recv()
            sl = pl.ds(way * C, C)
            part[j, d, sl] = (part[j, d, sl].astype(F32) + r1[j, way].astype(F32)).astype(BF16)
            stage2(j, way).start()

    def collect(j):
        stage2(j, 0).wait_recv()
        stage2(j, 1).wait_recv()
        total = part[j, head].astype(F32) + r2[j, 0].astype(F32) + r2[j, 1].astype(F32)
        csum[j] = total.astype(BF16)

    def final(c, k, side):
        there = (n_head - k) % n_head
        return send(
            give.at[c, k, side],
            take.at[c, there, cfg],
            f_send.at[c, k, side],
            f_recv.at[c, there, cfg],
            (lon, heads[k], side),
        )

    def final_in(c, k, side):
        return send(
            give.at[c, k, side], take.at[c, k, side], f_send.at[c, k, side], f_recv.at[c, k, side], to_hp
        )

    def finish(c):
        total = kept[c]
        for k in range(1, n_head):
            for side in range(2):
                final_in(c, k, side).wait_recv()
                total = total + take[c, k, side].astype(F32)
        final_in(c, 0, 1 - cfg).wait_recv()
        total = total + take[c, 0, 1 - cfg].astype(F32)
        out_ref[:, c] = total.reshape(frames, rows, half_feat).astype(out_ref.dtype)

    n_keys = (2 * cols + 1) * C

    def attend(branch, c, at):
        r0 = pl.multiple_of(c * C, C)
        for p in range(feat // PAIR):
            sl = pl.ds(p * PAIR, PAIR)
            att[pl.ds(at, C), sl] = attend_pair(
                q[branch, pl.ds(r0, C), sl],
                kv[branch, pl.ds(r0, n_keys), sl],
                kv[branch, pl.ds(r0, n_keys), pl.ds(feat + p * PAIR, PAIR)],
            )

    def wait_halo(branch, g, side):
        halo(branch, g, side, g * G).wait_recv()

    @pl.when(is_cond)
    def _():
        for g in range(groups):
            wait_halo(CTRL, g, 0)

        @pl.loop(0, groups)
        def _(j):
            wait_halo(CTRL, j, 1)
            for c in range(GROUP):
                attend(CTRL, j * GROUP + c, c * C)
            for d in range(n_head):
                part[j, d] = jnp.dot(att[...], wo[CTRL, d], preferred_element_type=F32).astype(BF16)
            stage1(j, 0).start()
            stage1(j, 1).start()

            @pl.when(j >= 1)
            def _():
                relay(j - 1)

            @pl.when(j >= 2)
            def _():
                collect(j - 2)

    for g in range(groups):
        wait_halo(BASE, g, 0)

    @pl.loop(0, cols)
    def _(c):
        @pl.when(lax.rem(c, GROUP) == 0)
        def _():
            wait_halo(BASE, lax.div(c, GROUP), 1)

        @pl.when(jnp.logical_and(is_cond, c == 1))
        def _():
            relay(groups - 1)
            collect(groups - 2)

        @pl.when(jnp.logical_and(is_cond, c == 3))
        def _():
            collect(groups - 1)

        attend(BASE, c, 0)
        for k in (2, 1, 3, 0):
            d = heads[k]
            val = jnp.dot(att[pl.ds(0, C), :], wo[BASE, d], preferred_element_type=F32)
            if k == 0:
                val += xg[head, :, c].reshape(C, feat).astype(F32)
            res = csum[lax.div(c, GROUP), pl.ds(pl.multiple_of(lax.rem(c, GROUP) * C, C), C), :]
            val += jnp.dot(res, wo[2, d], preferred_element_type=F32)
            val *= factor
            low, high = val[:, :half_feat], val[:, half_feat:]
            if k == 0:
                kept[c] = jnp.where(is_cond, low, high)
                give[c, 0, 1 - cfg] = jnp.where(is_cond, high, low).astype(BF16)
                final(c, 0, 1 - cfg).start()
            else:
                give[c, k, 0] = low.astype(BF16)
                give[c, k, 1] = high.astype(BF16)
                final(c, k, 0).start()
                final(c, k, 1).start()

        @pl.when(jnp.logical_and(is_cond, c >= 2))
        def _():
            finish(c - 2)

    @pl.loop(jnp.where(is_cond, cols - 2, 0), cols)
    def _(c):
        finish(c)

    for c in range(cols):
        own_send(c, 0, to_hp).wait_send()
        own_send(c, 1, to_hm).wait_send()
        gather(hm, c, 2, to_hp).wait_send()

    for g in range(groups):
        for side in range(2):
            halo(BASE, g, side, g * G).wait_send()

    @pl.when(is_cond)
    def _():
        for g in range(groups):
            for side in range(2):
                halo(CTRL, g, side, g * G).wait_send()
                stage1(g, side).wait_send()
                stage2(g, side).wait_send()

    @pl.loop(0, cols)
    def _(c):
        for k in range(1, n_head):
            for side in range(2):
                final(c, k, side).wait_send()
        final(c, 0, 1 - cfg).wait_send()


def local(
    latents,
    timestep,
    guide_num,
    guide_den,
    depth_level,
    depth_table,
    time_weight,
    base_q,
    base_k,
    base_v,
    base_o,
    ctrl_q,
    ctrl_k,
    ctrl_v,
    ctrl_o,
    zero_linear,
):
    x = latents[0].transpose(0, 2, 1, 3)
    frames, cols, rows, feat = x.shape
    n_lon, n_head = lax.axis_size("lon"), lax.axis_size("head")
    C, T, width = frames * rows, frames * rows * cols, feat * n_head
    freqs = jnp.exp(-math.log(10000.0) * jnp.arange(FREQ // 2).astype(F32) / (FREQ // 2))
    freqs = jnp.broadcast_to(freqs[None, :], (16, FREQ // 2))
    dma = pltpu.SemaphoreType.DMA
    vmem = pl.BlockSpec(memory_space=pltpu.VMEM)
    smem = pl.BlockSpec(memory_space=pltpu.SMEM)
    hbm = pl.BlockSpec(memory_space=pl.ANY)
    groups = cols // GROUP
    out = pl.pallas_call(
        functools.partial(kernel, (frames, rows, cols, feat, n_lon, n_head)),
        out_shape=jax.ShapeDtypeStruct((frames, cols, rows, feat // 2), BF16),
        in_specs=[hbm, smem, smem, smem, vmem, vmem, vmem] + [hbm] * 10,
        out_specs=vmem,
        scratch_shapes=[
            pltpu.VMEM((n_head, frames, cols, rows, feat), BF16),
            pltpu.VMEM((FREQ, 2 * width), BF16),
            pltpu.VMEM((2, width, 3 * feat), BF16),
            pltpu.VMEM((3, n_head, feat, feat), BF16),
            pltpu.VMEM((16, 2 * width), F32),
            pltpu.VMEM((2, GROUP * C, width), BF16),
            pltpu.VMEM((2, T, feat), BF16),
            pltpu.VMEM((2, 3 * T, 2 * feat), BF16),
            pltpu.VMEM((GROUP * C, feat), BF16),
            pltpu.VMEM((groups, GROUP * C, feat), BF16),
            pltpu.VMEM((groups, n_head, GROUP * C, feat), BF16),
            pltpu.VMEM((groups, 2, C, feat), BF16),
            pltpu.VMEM((groups, 2, GROUP * C, feat), BF16),
            pltpu.VMEM((cols, C, feat // 2), F32),
            pltpu.VMEM((cols, n_head, 2, C, feat // 2), BF16),
            pltpu.VMEM((cols, n_head, 2, C, feat // 2), BF16),
            dma((20,)),
            dma((3, cols)),
            dma((3, cols)),
            dma((2, groups, 2)),
            dma((2, groups, 2)),
            dma((groups, 2)),
            dma((groups, 2)),
            dma((groups, 2)),
            dma((groups, 2)),
            dma((cols, n_head, 2)),
            dma((cols, n_head, 2)),
        ],
        compiler_params=pltpu.CompilerParams(
            collective_id=0, has_side_effects=True, vmem_limit_bytes=58 * 1024 * 1024
        ),
    )(
        x,
        timestep,
        guide_num,
        guide_den,
        depth_level.transpose(2, 0, 1),
        freqs,
        depth_table,
        time_weight,
        base_q,
        base_k,
        base_v,
        base_o,
        ctrl_q,
        ctrl_k,
        ctrl_v,
        ctrl_o,
        zero_linear,
    )
    return out.transpose(0, 2, 1, 3)


def solution(mesh):
    return jax.shard_map(
        local,
        mesh=mesh,
        in_specs=(
            P("cfg", None, None, "lon", "head"),
            P(),
            P(),
            P(),
            P(None, None, "lon"),
            P(),
            P(),
            P(None, "head"),
            P(None, "head"),
            P(None, "head"),
            P("head", None),
            P(None, "head"),
            P(None, "head"),
            P(None, "head"),
            P("head", None),
            P("head", None),
        ),
        out_specs=P(None, None, "lon", ("head", "cfg")),
        check_vma=False,
    )
```

```python
import functools
import math

import jax
import jax.numpy as jnp
from jax import lax
from jax.experimental import pallas as pl
from jax.experimental.pallas import tpu as pltpu
from jax.sharding import PartitionSpec as P

HD = 64
FREQ = 256
PAIR = 2 * HD
GROUP = 2
BASE, CTRL = 0, 1
F32 = jnp.float32
BF16 = jnp.bfloat16
MESH = pl.DeviceIdType.MESH


def attend_pair(q, k, v):
    rows = q.shape[0]
    low = lax.broadcasted_iota(jnp.int32, (rows, PAIR), 1) < HD
    zero = jnp.zeros_like(q)
    both = jnp.concatenate([jnp.where(low, q, zero), jnp.where(low, zero, q)], axis=0)
    scores = lax.dot_general(both, k, (((1,), (1,)), ((), ())), preferred_element_type=F32)
    top = jnp.max(scores, axis=1, keepdims=True)
    expo = jnp.exp2(scores - top).astype(BF16)
    ones = jnp.concatenate([v, jnp.ones_like(v)], axis=1)
    mixed = jnp.dot(expo, ones, preferred_element_type=F32)
    mixed = mixed[:, :PAIR] / mixed[:, PAIR:]
    return jnp.where(low, mixed[:rows], mixed[rows:]).astype(BF16)


def kernel(
    dims,
    x_hbm,
    step_ref,
    num_ref,
    den_ref,
    level_ref,
    freq_ref,
    table_ref,
    tw_hbm,
    bq_hbm,
    bk_hbm,
    bv_hbm,
    bo_hbm,
    cq_hbm,
    ck_hbm,
    cv_hbm,
    co_hbm,
    zl_hbm,
    out_ref,
    xg,
    tw,
    wqkv,
    wo,
    mod,
    ms,
    q,
    kv,
    att,
    csum,
    part,
    parts_in,
    give,
    take,
    mine,
    swap_out,
    swap_in,
    load_sem,
    g_send,
    g_recv,
    h_send,
    h_recv,
    p_send,
    p_recv,
    f_send,
    f_recv,
    x_send,
    x_recv,
):
    frames, rows, cols, feat, n_lon, n_head = dims
    C = frames * rows
    T = C * cols
    width = feat * n_head
    groups = cols // GROUP
    G = GROUP * C
    lon, head, cfg = lax.axis_index("lon"), lax.axis_index("head"), lax.axis_index("cfg")
    is_cond = cfg == 0
    lp, lm = lax.rem(lon + 1, n_lon), lax.rem(lon + n_lon - 1, n_lon)
    to_lp, to_lm = (lp, head, cfg), (lm, head, cfg)
    half_feat = feat // 2
    heads = [head] + [lax.rem(head + k, n_head) for k in range(1, n_head)]
    peers = range(1, n_head)
    to_cfg = (lon, head, 1 - cfg)

    own_copy = pltpu.make_async_copy(x_hbm, xg.at[head], load_sem.at[0])
    own_copy.start()
    loads = [
        (tw_hbm, tw),
        (cq_hbm, wqkv.at[CTRL, :, pl.ds(0, feat)]),
        (ck_hbm, wqkv.at[CTRL, :, pl.ds(feat, feat)]),
        (cv_hbm, wqkv.at[CTRL, :, pl.ds(2 * feat, feat)]),
        (bq_hbm, wqkv.at[BASE, :, pl.ds(0, feat)]),
        (bk_hbm, wqkv.at[BASE, :, pl.ds(feat, feat)]),
        (bv_hbm, wqkv.at[BASE, :, pl.ds(2 * feat, feat)]),
    ]
    for at, w in ((CTRL, co_hbm), (BASE, bo_hbm), (2, zl_hbm)):
        loads += [(w.at[:, pl.ds(d * feat, feat)], wo.at[at, d]) for d in range(n_head)]
    loads = [pltpu.make_async_copy(s, d, load_sem.at[i + 1]) for i, (s, d) in enumerate(loads)]

    barrier = pltpu.get_barrier_semaphore()
    partners = [(lon, heads[k], cfg) for k in peers] + [to_cfg, to_lp, to_lm]
    for who in partners:
        pl.semaphore_signal(barrier, inc=1, device_id=who, device_id_type=MESH)
    for copy in loads:
        copy.start()
    pl.semaphore_wait(barrier, len(partners))

    def send(src, dst, ssem, rsem, who):
        return pltpu.make_async_remote_copy(
            src_ref=src, dst_ref=dst, send_sem=ssem, recv_sem=rsem, device_id=who, device_id_type=MESH
        )

    def to_peer(src, dst, ssem, rsem, k):
        return send(src, dst, ssem, rsem, (lon, heads[k], cfg))

    def gather(c, k):
        return to_peer(
            x_hbm.at[:, c], xg.at[head, :, c], g_send.at[k, c], g_recv.at[n_head - k, c], k
        )

    def gathered(c, k):
        return to_peer(x_hbm.at[:, c], xg.at[heads[k], :, c], g_send.at[k, c], g_recv.at[k, c], k)

    def halo(branch, g, side, row0):
        src = kv.at[branch, pl.ds(T + row0, G)]
        dst = kv.at[branch, pl.ds((0 if side == 0 else 2 * T) + row0, G)]
        who = to_lp if side == 0 else to_lm
        return send(src, dst, h_send.at[branch, g, side], h_recv.at[branch, g, side], who)

    def normalise(branch, c, at):
        parts = [xg[j, :, c].reshape(C, feat).astype(F32) for j in range(n_head)]
        if branch == CTRL:
            levels = lax.broadcasted_iota(jnp.int32, (table_ref.shape[0], rows), 0)
            hot = [jnp.where(levels == level_ref[c, f : f + 1, :], 1.0, 0.0).astype(BF16) for f in range(frames)]
            for j in range(n_head):
                table = table_ref[:, j * feat : (j + 1) * feat]
                emb = [
                    lax.dot_general(h, table, (((0,), (0,)), ((), ())), preferred_element_type=F32) for h in hot
                ]
                parts[j] = parts[j] + jnp.concatenate(emb, axis=0)
        center = sum(jnp.sum(u, axis=1, keepdims=True) for u in parts) * (1.0 / width)
        parts = [u - center for u in parts]
        spread = sum(jnp.sum(u * u, axis=1, keepdims=True) for u in parts) * (1.0 / width)
        scale = lax.rsqrt(spread + 1e-06)
        for j in range(n_head):
            sl = pl.ds(j * feat, feat)
            gain = 1.0 + mod[0:1, sl]
            shift = mod[0:1, pl.ds(width + j * feat, feat)]
            ms[branch, pl.ds(at, C), sl] = (parts[j] * scale * gain + shift).astype(BF16)

    def project(branch, g):
        for c in range(GROUP):
            normalise(branch, g * GROUP + c, c * C)
        row0 = g * G
        normed = ms[branch]
        query = jnp.dot(normed, wqkv[branch, :, :feat], preferred_element_type=F32)
        q[branch, pl.ds(row0, G), :] = (query * (math.log2(math.e) / math.sqrt(HD))).astype(BF16)
        kv[branch, pl.ds(T + row0, G), :] = jnp.dot(
            normed, wqkv[branch, :, feat:], preferred_element_type=F32
        ).astype(BF16)

    for c in range(cols):
        for k in (2, 1, 3):
            gather(c, k).start()

    @pl.when(jnp.logical_not(is_cond))
    def _():
        csum[...] = jnp.zeros_like(csum)

    angles = freq_ref[...] * step_ref[0].astype(F32)
    temb = jnp.concatenate([jnp.cos(angles), jnp.sin(angles)], axis=1).astype(BF16)
    loads[0].wait()
    mod[...] = jnp.dot(temb, tw[...], preferred_element_type=F32)
    ones = jnp.ones((8, feat), F32)
    ratio = (ones * num_ref[0].astype(F32)) / (ones * den_ref[0].astype(F32))
    factor = jnp.where(is_cond, ratio, 1.0 - ratio)[0:1, :]
    own_copy.wait()
    for copy in loads[1:]:
        copy.wait()

    for g in range(groups):
        for c in range(g * GROUP, (g + 1) * GROUP):
            for k in peers:
                gathered(c, k).wait_recv()

        @pl.when(is_cond)
        def _():
            project(CTRL, g)
            for side in range(2):
                halo(CTRL, g, side, g * G).start()

        project(BASE, g)

        @pl.when(jnp.logical_not(is_cond))
        def _():
            for side in range(2):
                halo(BASE, g, side, g * G).start()

    @pl.when(is_cond)
    def _():
        for g in range(groups):
            for side in range(2):
                halo(BASE, g, side, g * G).start()

    def ctrl_sum(j, k):
        return to_peer(part.at[j, k], parts_in.at[j, n_head - k], p_send.at[j, k], p_recv.at[j, n_head - k], k)

    def ctrl_in(j, k):
        return to_peer(part.at[j, k], parts_in.at[j, k], p_send.at[j, k], p_recv.at[j, k], k)

    def collect(j):
        total = part[j, 0].astype(F32)
        for k in peers:
            ctrl_in(j, k).wait_recv()
            total = total + parts_in[j, k].astype(F32)
        csum[j] = total.astype(BF16)

    def base_sum(c, k):
        return to_peer(give.at[c, k], take.at[c, n_head - k], f_send.at[c, k], f_recv.at[c, n_head - k], k)

    def base_in(c, k):
        return to_peer(give.at[c, k], take.at[c, k], f_send.at[c, k], f_recv.at[c, k], k)

    def swap(c):
        return send(swap_out.at[c], swap_in.at[c], x_send.at[c], x_recv.at[c], to_cfg)

    def reduce(c):
        total = give[c, 0].astype(F32) + xg[head, :, c].reshape(C, feat).astype(F32)
        for k in peers:
            base_in(c, k).wait_recv()
            total = total + take[c, k].astype(F32)
        total = total * factor
        low, high = total[:, :half_feat], total[:, half_feat:]
        mine[c] = jnp.where(is_cond, low, high)
        other = jnp.where(is_cond, high, low).astype(BF16)
        swap_out[c] = jnp.concatenate([other[: C // 2], other[C // 2 :]], axis=1)
        swap(c).start()

    def finish(c):
        swap(c).wait_recv()
        other = swap_in[c]
        other = jnp.concatenate([other[:, :half_feat], other[:, half_feat:]], axis=0)
        total = mine[c] + other.astype(F32)
        out_ref[:, c] = total.reshape(frames, rows, half_feat).astype(out_ref.dtype)

    n_keys = (2 * cols + 1) * C

    def attend(branch, c, at):
        r0 = pl.multiple_of(c * C, C)
        for p in range(feat // PAIR):
            sl = pl.ds(p * PAIR, PAIR)
            att[pl.ds(at, C), sl] = attend_pair(
                q[branch, pl.ds(r0, C), sl],
                kv[branch, pl.ds(r0, n_keys), sl],
                kv[branch, pl.ds(r0, n_keys), pl.ds(feat + p * PAIR, PAIR)],
            )

    def wait_halo(branch, g, side):
        halo(branch, g, side, g * G).wait_recv()

    @pl.when(is_cond)
    def _():
        for g in range(groups):
            wait_halo(CTRL, g, 0)

        @pl.loop(0, groups)
        def _(j):
            wait_halo(CTRL, j, 1)
            for c in range(GROUP):
                attend(CTRL, j * GROUP + c, c * C)
            for k in (2, 1, 3, 0):
                val = jnp.dot(att[...], wo[CTRL, heads[k]], preferred_element_type=F32)
                part[j, k] = val.astype(BF16)
                if k:
                    ctrl_sum(j, k).start()

            @pl.when(j >= 1)
            def _():
                collect(j - 1)

    for g in range(groups):
        wait_halo(BASE, g, 0)

    @pl.loop(0, cols)
    def _(c):
        @pl.when(lax.rem(c, GROUP) == 0)
        def _():
            wait_halo(BASE, lax.div(c, GROUP), 1)

        @pl.when(jnp.logical_and(is_cond, c == 3))
        def _():
            collect(groups - 1)

        attend(BASE, c, 0)
        res = csum[lax.div(c, GROUP), pl.ds(pl.multiple_of(lax.rem(c, GROUP) * C, C), C), :]
        for k in (2, 1, 3, 0):
            d = heads[k]
            val = jnp.dot(att[pl.ds(0, C), :], wo[BASE, d], preferred_element_type=F32)
            val += jnp.dot(res, wo[2, d], preferred_element_type=F32)
            give[c, k] = val.astype(BF16)
            if k:
                base_sum(c, k).start()

        @pl.when(c >= 2)
        def _():
            reduce(c - 2)

    reduce(cols - 2)
    reduce(cols - 1)

    @pl.loop(0, cols)
    def _(c):
        finish(c)

    for c in range(cols):
        for k in peers:
            gather(c, k).wait_send()

    for g in range(groups):
        for side in range(2):
            halo(BASE, g, side, g * G).wait_send()

    @pl.when(is_cond)
    def _():
        for g in range(groups):
            for side in range(2):
                halo(CTRL, g, side, g * G).wait_send()
            for k in peers:
                ctrl_sum(g, k).wait_send()

    @pl.loop(0, cols)
    def _(c):
        for k in peers:
            base_sum(c, k).wait_send()
        swap(c).wait_send()


def local(
    latents,
    timestep,
    guide_num,
    guide_den,
    depth_level,
    depth_table,
    time_weight,
    base_q,
    base_k,
    base_v,
    base_o,
    ctrl_q,
    ctrl_k,
    ctrl_v,
    ctrl_o,
    zero_linear,
):
    x = latents[0].transpose(0, 2, 1, 3)
    frames, cols, rows, feat = x.shape
    n_lon, n_head = lax.axis_size("lon"), lax.axis_size("head")
    C, T, width = frames * rows, frames * rows * cols, feat * n_head
    freqs = jnp.exp(-math.log(10000.0) * jnp.arange(FREQ // 2).astype(F32) / (FREQ // 2))
    freqs = jnp.broadcast_to(freqs[None, :], (16, FREQ // 2))
    dma = pltpu.SemaphoreType.DMA
    vmem = pl.BlockSpec(memory_space=pltpu.VMEM)
    smem = pl.BlockSpec(memory_space=pltpu.SMEM)
    hbm = pl.BlockSpec(memory_space=pl.ANY)
    groups = cols // GROUP
    out = pl.pallas_call(
        functools.partial(kernel, (frames, rows, cols, feat, n_lon, n_head)),
        out_shape=jax.ShapeDtypeStruct((frames, cols, rows, feat // 2), BF16),
        in_specs=[hbm, smem, smem, smem, vmem, vmem, vmem] + [hbm] * 10,
        out_specs=vmem,
        scratch_shapes=[
            pltpu.VMEM((n_head, frames, cols, rows, feat), BF16),
            pltpu.VMEM((FREQ, 2 * width), BF16),
            pltpu.VMEM((2, width, 3 * feat), BF16),
            pltpu.VMEM((3, n_head, feat, feat), BF16),
            pltpu.VMEM((16, 2 * width), F32),
            pltpu.VMEM((2, GROUP * C, width), BF16),
            pltpu.VMEM((2, T, feat), BF16),
            pltpu.VMEM((2, 3 * T, 2 * feat), BF16),
            pltpu.VMEM((GROUP * C, feat), BF16),
            pltpu.VMEM((groups, GROUP * C, feat), BF16),
            pltpu.VMEM((groups, n_head, GROUP * C, feat), BF16),
            pltpu.VMEM((groups, n_head, GROUP * C, feat), BF16),
            pltpu.VMEM((cols, n_head, C, feat), BF16),
            pltpu.VMEM((cols, n_head, C, feat), BF16),
            pltpu.VMEM((cols, C, feat // 2), F32),
            pltpu.VMEM((cols, C // 2, feat), BF16),
            pltpu.VMEM((cols, C // 2, feat), BF16),
            dma((20,)),
            dma((n_head, cols)),
            dma((n_head, cols)),
            dma((2, groups, 2)),
            dma((2, groups, 2)),
            dma((groups, n_head)),
            dma((groups, n_head)),
            dma((cols, n_head)),
            dma((cols, n_head)),
            dma((cols,)),
            dma((cols,)),
        ],
        compiler_params=pltpu.CompilerParams(
            collective_id=0, has_side_effects=True, vmem_limit_bytes=58 * 1024 * 1024
        ),
    )(
        x,
        timestep,
        guide_num,
        guide_den,
        depth_level.transpose(2, 0, 1),
        freqs,
        depth_table,
        time_weight,
        base_q,
        base_k,
        base_v,
        base_o,
        ctrl_q,
        ctrl_k,
        ctrl_v,
        ctrl_o,
        zero_linear,
    )
    return out.transpose(0, 2, 1, 3)


def solution(mesh):
    return jax.shard_map(
        local,
        mesh=mesh,
        in_specs=(
            P("cfg", None, None, "lon", "head"),
            P(),
            P(),
            P(),
            P(None, None, "lon"),
            P(),
            P(),
            P(None, "head"),
            P(None, "head"),
            P(None, "head"),
            P("head", None),
            P(None, "head"),
            P(None, "head"),
            P(None, "head"),
            P("head", None),
            P("head", None),
        ),
        out_specs=P(None, None, "lon", ("head", "cfg")),
        check_vma=False,
    )
```

```python
import functools
import math

import jax
import jax.numpy as jnp
from jax import lax
from jax.experimental import pallas as pl
from jax.experimental.pallas import tpu as pltpu
from jax.sharding import PartitionSpec as P

HD = 64
FREQ = 256
PAIR = 2 * HD
GROUP = 2
BASE, CTRL = 0, 1
F32 = jnp.float32
BF16 = jnp.bfloat16
MESH = pl.DeviceIdType.MESH


def attend_pair(q, k, v, count, near):
    rows = q.shape[0]
    C = rows // count
    total = k.shape[0]
    low = lax.broadcasted_iota(jnp.int32, (rows, PAIR), 1) < HD
    zero = jnp.zeros_like(q)
    both = jnp.concatenate([jnp.where(low, q, zero), jnp.where(low, zero, q)], axis=0)
    scores = lax.dot_general(both, k, (((1,), (1,)), ((), ())), preferred_element_type=F32)
    lane = lax.broadcasted_iota(jnp.int32, (C, 128), 1)
    weights = []
    for h in range(2):
        for b in range(count):
            r0 = (count * h + b) * C
            first, last = b * C, (b + near) * C
            t0, t1 = first // 128, -(-last // 128)
            tiles = []
            for t in range(t0, t1):
                at, end = t * 128, min(t * 128 + 128, total)
                tile = scores[r0 : r0 + C, at:end]
                if at < first:
                    tile = jnp.where(lane[:, : end - at] >= first - at, tile, -1e30)
                if end > last:
                    tile = jnp.where(lane[:, : end - at] < last - at, tile, -1e30)
                tiles.append(tile)
            row = jnp.concatenate(tiles, axis=1)
            top = jnp.max(row, axis=1, keepdims=True)
            expo = [jnp.exp2(row - top).astype(BF16)]
            if t0:
                expo = [jnp.zeros((C, t0 * 128), BF16)] + expo
            if t1 * 128 < total:
                expo = expo + [jnp.zeros((C, total - t1 * 128), BF16)]
            weights.append(jnp.concatenate(expo, axis=1) if len(expo) > 1 else expo[0])
    weights = jnp.concatenate(weights, axis=0)
    ones = jnp.concatenate([v, jnp.ones_like(v)], axis=1)
    mixed = jnp.dot(weights, ones, preferred_element_type=F32)
    mixed = mixed[:, :PAIR] / mixed[:, PAIR:]
    return jnp.where(low, mixed[:rows], mixed[rows:]).astype(BF16)


def kernel(
    dims,
    x_hbm,
    step_ref,
    num_ref,
    den_ref,
    level_ref,
    freq_ref,
    table_ref,
    tw_hbm,
    bq_hbm,
    bk_hbm,
    bv_hbm,
    bo_hbm,
    cq_hbm,
    ck_hbm,
    cv_hbm,
    co_hbm,
    zl_hbm,
    out_ref,
    xg,
    tw,
    wqkv,
    wo,
    mod,
    ms,
    q,
    kv,
    att,
    csum,
    part,
    parts_in,
    give,
    take,
    mine,
    swap_out,
    swap_in,
    load_sem,
    g_send,
    g_recv,
    h_send,
    h_recv,
    p_send,
    p_recv,
    f_send,
    f_recv,
    x_send,
    x_recv,
):
    frames, rows, cols, feat, n_lon, n_head = dims
    C = frames * rows
    T = C * cols
    width = feat * n_head
    groups = cols // GROUP
    G = GROUP * C
    lon, head, cfg = lax.axis_index("lon"), lax.axis_index("head"), lax.axis_index("cfg")
    is_cond = cfg == 0
    lp, lm = lax.rem(lon + 1, n_lon), lax.rem(lon + n_lon - 1, n_lon)
    to_lp, to_lm = (lp, head, cfg), (lm, head, cfg)
    half_feat = feat // 2
    heads = [head] + [lax.rem(head + k, n_head) for k in range(1, n_head)]
    peers = range(1, n_head)
    to_cfg = (lon, head, 1 - cfg)

    own_copy = pltpu.make_async_copy(x_hbm, xg.at[head], load_sem.at[0])
    own_copy.start()
    loads = [
        (tw_hbm, tw),
        (cq_hbm, wqkv.at[CTRL, :, pl.ds(0, feat)]),
        (ck_hbm, wqkv.at[CTRL, :, pl.ds(feat, feat)]),
        (cv_hbm, wqkv.at[CTRL, :, pl.ds(2 * feat, feat)]),
        (bq_hbm, wqkv.at[BASE, :, pl.ds(0, feat)]),
        (bk_hbm, wqkv.at[BASE, :, pl.ds(feat, feat)]),
        (bv_hbm, wqkv.at[BASE, :, pl.ds(2 * feat, feat)]),
    ]
    for at, w in ((CTRL, co_hbm), (BASE, bo_hbm), (2, zl_hbm)):
        loads += [(w.at[:, pl.ds(d * feat, feat)], wo.at[at, d]) for d in range(n_head)]
    loads = [pltpu.make_async_copy(s, d, load_sem.at[i + 1]) for i, (s, d) in enumerate(loads)]

    barrier = pltpu.get_barrier_semaphore()
    partners = [(lon, heads[k], cfg) for k in peers] + [to_cfg, to_lp, to_lm]
    for who in partners:
        pl.semaphore_signal(barrier, inc=1, device_id=who, device_id_type=MESH)
    for copy in loads:
        copy.start()
    pl.semaphore_wait(barrier, len(partners))

    def send(src, dst, ssem, rsem, who):
        return pltpu.make_async_remote_copy(
            src_ref=src, dst_ref=dst, send_sem=ssem, recv_sem=rsem, device_id=who, device_id_type=MESH
        )

    def to_peer(src, dst, ssem, rsem, k):
        return send(src, dst, ssem, rsem, (lon, heads[k], cfg))

    def gather(c, k):
        return to_peer(
            x_hbm.at[:, c], xg.at[head, :, c], g_send.at[k, c], g_recv.at[n_head - k, c], k
        )

    def gathered(c, k):
        return to_peer(x_hbm.at[:, c], xg.at[heads[k], :, c], g_send.at[k, c], g_recv.at[k, c], k)

    def halo(branch, g, side, row0):
        src = kv.at[branch, pl.ds(T + row0, G)]
        dst = kv.at[branch, pl.ds((0 if side == 0 else 2 * T) + row0, G)]
        who = to_lp if side == 0 else to_lm
        return send(src, dst, h_send.at[branch, g, side], h_recv.at[branch, g, side], who)

    def normalise(branch, c, at):
        parts = [xg[j, :, c].reshape(C, feat).astype(F32) for j in range(n_head)]
        if branch == CTRL:
            levels = lax.broadcasted_iota(jnp.int32, (table_ref.shape[0], rows), 0)
            hot = [jnp.where(levels == level_ref[c, f : f + 1, :], 1.0, 0.0).astype(BF16) for f in range(frames)]
            for j in range(n_head):
                table = table_ref[:, j * feat : (j + 1) * feat]
                emb = [
                    lax.dot_general(h, table, (((0,), (0,)), ((), ())), preferred_element_type=F32) for h in hot
                ]
                parts[j] = parts[j] + jnp.concatenate(emb, axis=0)
        center = sum(jnp.sum(u, axis=1, keepdims=True) for u in parts) * (1.0 / width)
        parts = [u - center for u in parts]
        spread = sum(jnp.sum(u * u, axis=1, keepdims=True) for u in parts) * (1.0 / width)
        scale = lax.rsqrt(spread + 1e-06)
        for j in range(n_head):
            sl = pl.ds(j * feat, feat)
            gain = 1.0 + mod[0:1, sl]
            shift = mod[0:1, pl.ds(width + j * feat, feat)]
            ms[branch, pl.ds(at, C), sl] = (parts[j] * scale * gain + shift).astype(BF16)

    def project(branch, g):
        for c in range(GROUP):
            normalise(branch, g * GROUP + c, c * C)
        row0 = g * G
        normed = ms[branch]
        query = jnp.dot(normed, wqkv[branch, :, :feat], preferred_element_type=F32)
        q[branch, pl.ds(row0, G), :] = (query * (math.log2(math.e) / math.sqrt(HD))).astype(BF16)
        kv[branch, pl.ds(T + row0, G), :] = jnp.dot(
            normed, wqkv[branch, :, feat:], preferred_element_type=F32
        ).astype(BF16)

    for c in range(cols):
        for k in (2, 1, 3):
            gather(c, k).start()

    @pl.when(jnp.logical_not(is_cond))
    def _():
        csum[...] = jnp.zeros_like(csum)

    angles = freq_ref[...] * step_ref[0].astype(F32)
    temb = jnp.concatenate([jnp.cos(angles), jnp.sin(angles)], axis=1).astype(BF16)
    loads[0].wait()
    mod[...] = jnp.dot(temb, tw[...], preferred_element_type=F32)
    ones = jnp.ones((8, feat), F32)
    ratio = (ones * num_ref[0].astype(F32)) / (ones * den_ref[0].astype(F32))
    factor = jnp.where(is_cond, ratio, 1.0 - ratio)[0:1, :]
    own_copy.wait()
    for copy in loads[1:]:
        copy.wait()

    for g in range(groups):
        for c in range(g * GROUP, (g + 1) * GROUP):
            for k in peers:
                gathered(c, k).wait_recv()

        @pl.when(is_cond)
        def _():
            project(CTRL, g)
            for side in range(2):
                halo(CTRL, g, side, g * G).start()

        project(BASE, g)

        @pl.when(jnp.logical_not(is_cond))
        def _():
            for side in range(2):
                halo(BASE, g, side, g * G).start()

    @pl.when(is_cond)
    def _():
        for g in range(groups):
            for side in range(2):
                halo(BASE, g, side, g * G).start()

    def ctrl_sum(j, k):
        return to_peer(part.at[j, k], parts_in.at[j, n_head - k], p_send.at[j, k], p_recv.at[j, n_head - k], k)

    def ctrl_in(j, k):
        return to_peer(part.at[j, k], parts_in.at[j, k], p_send.at[j, k], p_recv.at[j, k], k)

    def collect(j):
        total = part[j, 0].astype(F32)
        for k in peers:
            ctrl_in(j, k).wait_recv()
            total = total + parts_in[j, k].astype(F32)
        csum[j] = total.astype(BF16)

    def base_sum(c, k):
        return to_peer(give.at[c, k], take.at[c, n_head - k], f_send.at[c, k], f_recv.at[c, n_head - k], k)

    def base_in(c, k):
        return to_peer(give.at[c, k], take.at[c, k], f_send.at[c, k], f_recv.at[c, k], k)

    def swap(c):
        return send(swap_out.at[c], swap_in.at[c], x_send.at[c], x_recv.at[c], to_cfg)

    def reduce(c):
        total = give[c, 0].astype(F32) + xg[head, :, c].reshape(C, feat).astype(F32)
        for k in peers:
            base_in(c, k).wait_recv()
            total = total + take[c, k].astype(F32)
        total = total * factor
        low, high = total[:, :half_feat], total[:, half_feat:]
        mine[c] = jnp.where(is_cond, low, high)
        other = jnp.where(is_cond, high, low).astype(BF16)
        swap_out[c] = jnp.concatenate([other[: C // 2], other[C // 2 :]], axis=1)
        swap(c).start()

    def finish(c):
        swap(c).wait_recv()
        other = swap_in[c]
        other = jnp.concatenate([other[:, :half_feat], other[:, half_feat:]], axis=0)
        total = mine[c] + other.astype(F32)
        out_ref[:, c] = total.reshape(frames, rows, half_feat).astype(out_ref.dtype)

    near = 2 * cols + 1
    n_keys = (near + GROUP - 1) * C

    def attend(branch, j):
        r0 = j * G
        for p in range(feat // PAIR):
            sl = pl.ds(p * PAIR, PAIR)
            att[:, sl] = attend_pair(
                q[branch, pl.ds(r0, G), sl],
                kv[branch, pl.ds(r0, n_keys), sl],
                kv[branch, pl.ds(r0, n_keys), pl.ds(feat + p * PAIR, PAIR)],
                GROUP,
                near,
            )

    def wait_halo(branch, g, side):
        halo(branch, g, side, g * G).wait_recv()

    @pl.when(is_cond)
    def _():
        for g in range(groups):
            wait_halo(CTRL, g, 0)

        for j in range(groups):
            wait_halo(CTRL, j, 1)
            attend(CTRL, j)
            for k in (2, 1, 3, 0):
                val = jnp.dot(att[...], wo[CTRL, heads[k]], preferred_element_type=F32)
                part[j, k] = val.astype(BF16)
                if k:
                    ctrl_sum(j, k).start()
            if j >= 1:
                collect(j - 1)

    for g in range(groups):
        wait_halo(BASE, g, 0)

    for j in range(groups):
        wait_halo(BASE, j, 1)
        attend(BASE, j)

        if j == groups - 1:

            @pl.when(is_cond)
            def _():
                collect(groups - 1)

        for k in (2, 1, 3, 0):
            d = heads[k]
            val = jnp.dot(att[...], wo[BASE, d], preferred_element_type=F32)
            val += jnp.dot(csum[j], wo[2, d], preferred_element_type=F32)
            for b in range(GROUP):
                c = j * GROUP + b
                give[c, k] = val[b * C : (b + 1) * C].astype(BF16)
                if k:
                    base_sum(c, k).start()

        if j >= 1:
            for b in range(GROUP):
                reduce((j - 1) * GROUP + b)

    for b in range(GROUP):
        reduce(cols - GROUP + b)

    @pl.loop(0, cols)
    def _(c):
        finish(c)

    for c in range(cols):
        for k in peers:
            gather(c, k).wait_send()

    for g in range(groups):
        for side in range(2):
            halo(BASE, g, side, g * G).wait_send()

    @pl.when(is_cond)
    def _():
        for g in range(groups):
            for side in range(2):
                halo(CTRL, g, side, g * G).wait_send()
            for k in peers:
                ctrl_sum(g, k).wait_send()

    @pl.loop(0, cols)
    def _(c):
        for k in peers:
            base_sum(c, k).wait_send()
        swap(c).wait_send()


def local(
    latents,
    timestep,
    guide_num,
    guide_den,
    depth_level,
    depth_table,
    time_weight,
    base_q,
    base_k,
    base_v,
    base_o,
    ctrl_q,
    ctrl_k,
    ctrl_v,
    ctrl_o,
    zero_linear,
):
    x = latents[0].transpose(0, 2, 1, 3)
    frames, cols, rows, feat = x.shape
    n_lon, n_head = lax.axis_size("lon"), lax.axis_size("head")
    C, T, width = frames * rows, frames * rows * cols, feat * n_head
    freqs = jnp.exp(-math.log(10000.0) * jnp.arange(FREQ // 2).astype(F32) / (FREQ // 2))
    freqs = jnp.broadcast_to(freqs[None, :], (16, FREQ // 2))
    dma = pltpu.SemaphoreType.DMA
    vmem = pl.BlockSpec(memory_space=pltpu.VMEM)
    smem = pl.BlockSpec(memory_space=pltpu.SMEM)
    hbm = pl.BlockSpec(memory_space=pl.ANY)
    groups = cols // GROUP
    out = pl.pallas_call(
        functools.partial(kernel, (frames, rows, cols, feat, n_lon, n_head)),
        out_shape=jax.ShapeDtypeStruct((frames, cols, rows, feat // 2), BF16),
        in_specs=[hbm, smem, smem, smem, vmem, vmem, vmem] + [hbm] * 10,
        out_specs=vmem,
        scratch_shapes=[
            pltpu.VMEM((n_head, frames, cols, rows, feat), BF16),
            pltpu.VMEM((FREQ, 2 * width), BF16),
            pltpu.VMEM((2, width, 3 * feat), BF16),
            pltpu.VMEM((3, n_head, feat, feat), BF16),
            pltpu.VMEM((16, 2 * width), F32),
            pltpu.VMEM((2, GROUP * C, width), BF16),
            pltpu.VMEM((2, T, feat), BF16),
            pltpu.VMEM((2, 3 * T, 2 * feat), BF16),
            pltpu.VMEM((GROUP * C, feat), BF16),
            pltpu.VMEM((groups, GROUP * C, feat), BF16),
            pltpu.VMEM((groups, n_head, GROUP * C, feat), BF16),
            pltpu.VMEM((groups, n_head, GROUP * C, feat), BF16),
            pltpu.VMEM((cols, n_head, C, feat), BF16),
            pltpu.VMEM((cols, n_head, C, feat), BF16),
            pltpu.VMEM((cols, C, feat // 2), F32),
            pltpu.VMEM((cols, C // 2, feat), BF16),
            pltpu.VMEM((cols, C // 2, feat), BF16),
            dma((20,)),
            dma((n_head, cols)),
            dma((n_head, cols)),
            dma((2, groups, 2)),
            dma((2, groups, 2)),
            dma((groups, n_head)),
            dma((groups, n_head)),
            dma((cols, n_head)),
            dma((cols, n_head)),
            dma((cols,)),
            dma((cols,)),
        ],
        compiler_params=pltpu.CompilerParams(
            collective_id=0, has_side_effects=True, vmem_limit_bytes=58 * 1024 * 1024
        ),
    )(
        x,
        timestep,
        guide_num,
        guide_den,
        depth_level.transpose(2, 0, 1),
        freqs,
        depth_table,
        time_weight,
        base_q,
        base_k,
        base_v,
        base_o,
        ctrl_q,
        ctrl_k,
        ctrl_v,
        ctrl_o,
        zero_linear,
    )
    return out.transpose(0, 2, 1, 3)


def solution(mesh):
    return jax.shard_map(
        local,
        mesh=mesh,
        in_specs=(
            P("cfg", None, None, "lon", "head"),
            P(),
            P(),
            P(),
            P(None, None, "lon"),
            P(),
            P(),
            P(None, "head"),
            P(None, "head"),
            P(None, "head"),
            P("head", None),
            P(None, "head"),
            P(None, "head"),
            P(None, "head"),
            P("head", None),
            P("head", None),
        ),
        out_specs=P(None, None, "lon", ("head", "cfg")),
        check_vma=False,
    )
```

```python
import functools
import math

import jax
import jax.numpy as jnp
from jax import lax
from jax.experimental import pallas as pl
from jax.experimental.pallas import tpu as pltpu
from jax.sharding import PartitionSpec as P

HD = 64
FREQ = 256
PAIR = 2 * HD
GROUP = 2
BASE, CTRL = 0, 1
F32 = jnp.float32
BF16 = jnp.bfloat16
MESH = pl.DeviceIdType.MESH


def attend_pair(q, k, v, count, near):
    rows = q.shape[0]
    C = rows // count
    total = k.shape[0]
    low = lax.broadcasted_iota(jnp.int32, (rows, PAIR), 1) < HD
    zero = jnp.zeros_like(q)
    both = jnp.concatenate([jnp.where(low, q, zero), jnp.where(low, zero, q)], axis=0)
    scores = lax.dot_general(both, k, (((1,), (1,)), ((), ())), preferred_element_type=F32)
    lane = lax.broadcasted_iota(jnp.int32, (C, 128), 1)
    weights = []
    for h in range(2):
        for b in range(count):
            r0 = (count * h + b) * C
            first, last = b * C, (b + near) * C
            t0, t1 = first // 128, -(-last // 128)
            tiles = []
            for t in range(t0, t1):
                at, end = t * 128, min(t * 128 + 128, total)
                tile = scores[r0 : r0 + C, at:end]
                if at < first:
                    tile = jnp.where(lane[:, : end - at] >= first - at, tile, -1e30)
                if end > last:
                    tile = jnp.where(lane[:, : end - at] < last - at, tile, -1e30)
                tiles.append(tile)
            row = jnp.concatenate(tiles, axis=1)
            top = jnp.max(row, axis=1, keepdims=True)
            expo = [jnp.exp2(row - top).astype(BF16)]
            if t0:
                expo = [jnp.zeros((C, t0 * 128), BF16)] + expo
            if t1 * 128 < total:
                expo = expo + [jnp.zeros((C, total - t1 * 128), BF16)]
            weights.append(jnp.concatenate(expo, axis=1) if len(expo) > 1 else expo[0])
    weights = jnp.concatenate(weights, axis=0)
    ones = jnp.concatenate([v, jnp.ones_like(v)], axis=1)
    mixed = jnp.dot(weights, ones, preferred_element_type=F32)
    mixed = mixed[:, :PAIR] / mixed[:, PAIR:]
    return jnp.where(low, mixed[:rows], mixed[rows:]).astype(BF16)


def kernel(
    dims,
    x_hbm,
    step_ref,
    num_ref,
    den_ref,
    level_ref,
    freq_ref,
    table_ref,
    tw_hbm,
    bq_hbm,
    bk_hbm,
    bv_hbm,
    bo_hbm,
    cq_hbm,
    ck_hbm,
    cv_hbm,
    co_hbm,
    zl_hbm,
    out_ref,
    xg,
    tw,
    wqkv,
    wo,
    mod,
    ms,
    q,
    kv,
    att,
    csum,
    part,
    parts_in,
    give,
    take,
    mine,
    swap_out,
    swap_in,
    load_sem,
    g_send,
    g_recv,
    h_send,
    h_recv,
    p_send,
    p_recv,
    f_send,
    f_recv,
    x_send,
    x_recv,
):
    frames, rows, cols, feat, n_lon, n_head = dims
    C = frames * rows
    T = C * cols
    width = feat * n_head
    groups = cols // GROUP
    G = GROUP * C
    lon, head, cfg = lax.axis_index("lon"), lax.axis_index("head"), lax.axis_index("cfg")
    is_cond = cfg == 0
    lp, lm = lax.rem(lon + 1, n_lon), lax.rem(lon + n_lon - 1, n_lon)
    to_lp, to_lm = (lp, head, cfg), (lm, head, cfg)
    half_feat = feat // 2
    core = lax.rem(lon, 2)
    make = [jnp.where(core == 0, g, groups - 1 - g) for g in range(groups)]
    order = [jnp.where(core == 0, groups - 1 - g, g) for g in range(groups)]
    make_cols = [jnp.where(core == 0, c, cols - 1 - c) for c in range(cols)]
    heads = [head] + [lax.rem(head + k, n_head) for k in range(1, n_head)]
    peers = range(1, n_head)
    to_cfg = (lon, head, 1 - cfg)

    own_copy = pltpu.make_async_copy(x_hbm, xg.at[head], load_sem.at[0])
    own_copy.start()
    loads = [
        (tw_hbm, tw),
        (cq_hbm, wqkv.at[CTRL, :, pl.ds(0, feat)]),
        (ck_hbm, wqkv.at[CTRL, :, pl.ds(feat, feat)]),
        (cv_hbm, wqkv.at[CTRL, :, pl.ds(2 * feat, feat)]),
        (bq_hbm, wqkv.at[BASE, :, pl.ds(0, feat)]),
        (bk_hbm, wqkv.at[BASE, :, pl.ds(feat, feat)]),
        (bv_hbm, wqkv.at[BASE, :, pl.ds(2 * feat, feat)]),
    ]
    for at, w in ((CTRL, co_hbm), (BASE, bo_hbm), (2, zl_hbm)):
        loads += [(w.at[:, pl.ds(d * feat, feat)], wo.at[at, d]) for d in range(n_head)]
    loads = [pltpu.make_async_copy(s, d, load_sem.at[i + 1]) for i, (s, d) in enumerate(loads)]

    barrier = pltpu.get_barrier_semaphore()
    partners = [(lon, heads[k], cfg) for k in peers] + [to_cfg, to_lp, to_lm]
    for who in partners:
        pl.semaphore_signal(barrier, inc=1, device_id=who, device_id_type=MESH)
    for copy in loads:
        copy.start()
    pl.semaphore_wait(barrier, len(partners))

    def send(src, dst, ssem, rsem, who):
        return pltpu.make_async_remote_copy(
            src_ref=src, dst_ref=dst, send_sem=ssem, recv_sem=rsem, device_id=who, device_id_type=MESH
        )

    def to_peer(src, dst, ssem, rsem, k):
        return send(src, dst, ssem, rsem, (lon, heads[k], cfg))

    def gather(c, k):
        return to_peer(
            x_hbm.at[:, c], xg.at[head, :, c], g_send.at[k, c], g_recv.at[n_head - k, c], k
        )

    def gathered(c, k):
        return to_peer(x_hbm.at[:, c], xg.at[heads[k], :, c], g_send.at[k, c], g_recv.at[k, c], k)

    def own_rows(g):
        return pl.ds(pl.multiple_of(T + g * G, G), G)

    def halo(branch, g, side):
        dst = pl.ds(pl.multiple_of((0 if side == 0 else 2 * T) + g * G, G), G)
        who = to_lp if side == 0 else to_lm
        return send(
            kv.at[branch, own_rows(g)], kv.at[branch, dst], h_send.at[branch, g, side], h_recv.at[branch, g, side], who
        )

    def wait_halo(branch, g, side):
        dst = pl.ds(pl.multiple_of(2 * T * side + g * G, G), G)
        send(
            kv.at[branch, own_rows(g)], kv.at[branch, dst], h_send.at[branch, g, side], h_recv.at[branch, g, side], to_lp
        ).wait_recv()

    def normalise(branch, c, at):
        parts = [xg[j, :, c].reshape(C, feat).astype(F32) for j in range(n_head)]
        if branch == CTRL:
            levels = lax.broadcasted_iota(jnp.int32, (table_ref.shape[0], rows), 0)
            hot = [jnp.where(levels == level_ref[c, f : f + 1, :], 1.0, 0.0).astype(BF16) for f in range(frames)]
            for j in range(n_head):
                table = table_ref[:, j * feat : (j + 1) * feat]
                emb = [
                    lax.dot_general(h, table, (((0,), (0,)), ((), ())), preferred_element_type=F32) for h in hot
                ]
                parts[j] = parts[j] + jnp.concatenate(emb, axis=0)
        center = sum(jnp.sum(u, axis=1, keepdims=True) for u in parts) * (1.0 / width)
        parts = [u - center for u in parts]
        spread = sum(jnp.sum(u * u, axis=1, keepdims=True) for u in parts) * (1.0 / width)
        scale = lax.rsqrt(spread + 1e-06)
        for j in range(n_head):
            sl = pl.ds(j * feat, feat)
            gain = 1.0 + mod[0:1, sl]
            shift = mod[0:1, pl.ds(width + j * feat, feat)]
            ms[branch, pl.ds(at, C), sl] = (parts[j] * scale * gain + shift).astype(BF16)

    def project(branch, g):
        for c in range(GROUP):
            normalise(branch, g * GROUP + c, c * C)
        normed = ms[branch]
        kv[branch, own_rows(g), :] = jnp.dot(
            normed, wqkv[branch, :, feat:], preferred_element_type=F32
        ).astype(BF16)
        for side in range(2):
            halo(branch, g, side).start()
        query = jnp.dot(normed, wqkv[branch, :, :feat], preferred_element_type=F32)
        q[branch, pl.ds(pl.multiple_of(g * G, G), G), :] = (query * (math.log2(math.e) / math.sqrt(HD))).astype(BF16)

    for c in make_cols:
        for k in (2, 1, 3):
            gather(c, k).start()

    @pl.when(jnp.logical_not(is_cond))
    def _():
        csum[...] = jnp.zeros_like(csum)

    angles = freq_ref[...] * step_ref[0].astype(F32)
    temb = jnp.concatenate([jnp.cos(angles), jnp.sin(angles)], axis=1).astype(BF16)
    loads[0].wait()
    mod[...] = jnp.dot(temb, tw[...], preferred_element_type=F32)
    ones = jnp.ones((8, feat), F32)
    ratio = (ones * num_ref[0].astype(F32)) / (ones * den_ref[0].astype(F32))
    factor = jnp.where(is_cond, ratio, 1.0 - ratio)[0:1, :]
    own_copy.wait()
    for copy in loads[1:]:
        copy.wait()

    for i, g in enumerate(make):
        for c in make_cols[i * GROUP : (i + 1) * GROUP]:
            for k in peers:
                gathered(c, k).wait_recv()

        @pl.when(is_cond)
        def _():
            project(CTRL, g)

        project(BASE, g)

    def ctrl_sum(j, k):
        return to_peer(part.at[j, k], parts_in.at[j, n_head - k], p_send.at[j, k], p_recv.at[j, n_head - k], k)

    def ctrl_in(j, k):
        return to_peer(part.at[j, k], parts_in.at[j, k], p_send.at[j, k], p_recv.at[j, k], k)

    def collect(j):
        total = part[j, 0].astype(F32)
        for k in peers:
            ctrl_in(j, k).wait_recv()
            total = total + parts_in[j, k].astype(F32)
        csum[j] = total.astype(BF16)

    def base_sum(c, k):
        return to_peer(give.at[c, k], take.at[c, n_head - k], f_send.at[c, k], f_recv.at[c, n_head - k], k)

    def base_in(c, k):
        return to_peer(give.at[c, k], take.at[c, k], f_send.at[c, k], f_recv.at[c, k], k)

    def swap(c):
        return send(swap_out.at[c], swap_in.at[c], x_send.at[c], x_recv.at[c], to_cfg)

    def reduce(c):
        total = give[c, 0].astype(F32) + xg[head, :, c].reshape(C, feat).astype(F32)
        for k in peers:
            base_in(c, k).wait_recv()
            total = total + take[c, k].astype(F32)
        total = total * factor
        low, high = total[:, :half_feat], total[:, half_feat:]
        mine[c] = jnp.where(is_cond, low, high)
        other = jnp.where(is_cond, high, low).astype(BF16)
        swap_out[c] = jnp.concatenate([other[: C // 2], other[C // 2 :]], axis=1)
        swap(c).start()

    def finish(c):
        swap(c).wait_recv()
        other = swap_in[c]
        other = jnp.concatenate([other[:, :half_feat], other[:, half_feat:]], axis=0)
        total = mine[c] + other.astype(F32)
        out_ref[:, c] = total.reshape(frames, rows, half_feat).astype(out_ref.dtype)

    near = 2 * cols + 1
    n_keys = (near + GROUP - 1) * C

    def attend(branch, j):
        r0 = pl.multiple_of(j * G, G)
        for p in range(feat // PAIR):
            sl = pl.ds(p * PAIR, PAIR)
            att[:, sl] = attend_pair(
                q[branch, pl.ds(r0, G), sl],
                kv[branch, pl.ds(r0, n_keys), sl],
                kv[branch, pl.ds(r0, n_keys), pl.ds(feat + p * PAIR, PAIR)],
                GROUP,
                near,
            )

    @pl.when(is_cond)
    def _():
        for g in range(groups):
            wait_halo(CTRL, g, 1 - core)

        for j in order:
            wait_halo(CTRL, j, core)
            attend(CTRL, j)
            for k in (2, 1, 3, 0):
                val = jnp.dot(att[...], wo[CTRL, heads[k]], preferred_element_type=F32)
                part[j, k] = val.astype(BF16)
                if k:
                    ctrl_sum(j, k).start()

    for g in range(groups):
        wait_halo(BASE, g, 1 - core)

    def reduce_unit(j):
        for b in range(GROUP):
            reduce(j * GROUP + b)

    for i, j in enumerate(order):
        wait_halo(BASE, j, core)
        attend(BASE, j)

        @pl.when(is_cond)
        def _():
            collect(j)

        for k in (2, 1, 3, 0):
            d = heads[k]
            val = jnp.dot(att[...], wo[BASE, d], preferred_element_type=F32)
            val += jnp.dot(csum[j], wo[2, d], preferred_element_type=F32)
            for b in range(GROUP):
                c = j * GROUP + b
                give[c, k] = val[b * C : (b + 1) * C].astype(BF16)
                if k:
                    base_sum(c, k).start()

        if i >= 2:
            reduce_unit(order[i - 2])

    for j in order[groups - 2 :]:
        reduce_unit(j)

    for j in order:
        for b in range(GROUP):
            finish(j * GROUP + b)

    for c in range(cols):
        for k in peers:
            gather(c, k).wait_send()

    for g in range(groups):
        for side in range(2):
            halo(BASE, g, side).wait_send()

    @pl.when(is_cond)
    def _():
        for g in range(groups):
            for side in range(2):
                halo(CTRL, g, side).wait_send()
            for k in peers:
                ctrl_sum(g, k).wait_send()

    @pl.loop(0, cols)
    def _(c):
        for k in peers:
            base_sum(c, k).wait_send()
        swap(c).wait_send()


def local(
    latents,
    timestep,
    guide_num,
    guide_den,
    depth_level,
    depth_table,
    time_weight,
    base_q,
    base_k,
    base_v,
    base_o,
    ctrl_q,
    ctrl_k,
    ctrl_v,
    ctrl_o,
    zero_linear,
):
    x = latents[0].transpose(0, 2, 1, 3)
    frames, cols, rows, feat = x.shape
    n_lon, n_head = lax.axis_size("lon"), lax.axis_size("head")
    C, T, width = frames * rows, frames * rows * cols, feat * n_head
    freqs = jnp.exp(-math.log(10000.0) * jnp.arange(FREQ // 2).astype(F32) / (FREQ // 2))
    freqs = jnp.broadcast_to(freqs[None, :], (16, FREQ // 2))
    dma = pltpu.SemaphoreType.DMA
    vmem = pl.BlockSpec(memory_space=pltpu.VMEM)
    smem = pl.BlockSpec(memory_space=pltpu.SMEM)
    hbm = pl.BlockSpec(memory_space=pl.ANY)
    groups = cols // GROUP
    out = pl.pallas_call(
        functools.partial(kernel, (frames, rows, cols, feat, n_lon, n_head)),
        out_shape=jax.ShapeDtypeStruct((frames, cols, rows, feat // 2), BF16),
        in_specs=[hbm, smem, smem, smem, vmem, vmem, vmem] + [hbm] * 10,
        out_specs=vmem,
        scratch_shapes=[
            pltpu.VMEM((n_head, frames, cols, rows, feat), BF16),
            pltpu.VMEM((FREQ, 2 * width), BF16),
            pltpu.VMEM((2, width, 3 * feat), BF16),
            pltpu.VMEM((3, n_head, feat, feat), BF16),
            pltpu.VMEM((16, 2 * width), F32),
            pltpu.VMEM((2, GROUP * C, width), BF16),
            pltpu.VMEM((2, T, feat), BF16),
            pltpu.VMEM((2, 3 * T, 2 * feat), BF16),
            pltpu.VMEM((GROUP * C, feat), BF16),
            pltpu.VMEM((groups, GROUP * C, feat), BF16),
            pltpu.VMEM((groups, n_head, GROUP * C, feat), BF16),
            pltpu.VMEM((groups, n_head, GROUP * C, feat), BF16),
            pltpu.VMEM((cols, n_head, C, feat), BF16),
            pltpu.VMEM((cols, n_head, C, feat), BF16),
            pltpu.VMEM((cols, C, feat // 2), F32),
            pltpu.VMEM((cols, C // 2, feat), BF16),
            pltpu.VMEM((cols, C // 2, feat), BF16),
            dma((20,)),
            dma((n_head, cols)),
            dma((n_head, cols)),
            dma((2, groups, 2)),
            dma((2, groups, 2)),
            dma((groups, n_head)),
            dma((groups, n_head)),
            dma((cols, n_head)),
            dma((cols, n_head)),
            dma((cols,)),
            dma((cols,)),
        ],
        compiler_params=pltpu.CompilerParams(
            collective_id=0, has_side_effects=True, vmem_limit_bytes=58 * 1024 * 1024
        ),
    )(
        x,
        timestep,
        guide_num,
        guide_den,
        depth_level.transpose(2, 0, 1),
        freqs,
        depth_table,
        time_weight,
        base_q,
        base_k,
        base_v,
        base_o,
        ctrl_q,
        ctrl_k,
        ctrl_v,
        ctrl_o,
        zero_linear,
    )
    return out.transpose(0, 2, 1, 3)


def solution(mesh):
    return jax.shard_map(
        local,
        mesh=mesh,
        in_specs=(
            P("cfg", None, None, "lon", "head"),
            P(),
            P(),
            P(),
            P(None, None, "lon"),
            P(),
            P(),
            P(None, "head"),
            P(None, "head"),
            P(None, "head"),
            P("head", None),
            P(None, "head"),
            P(None, "head"),
            P(None, "head"),
            P("head", None),
            P("head", None),
        ),
        out_specs=P(None, None, "lon", ("head", "cfg")),
        check_vma=False,
    )
```

```python
import functools
import math

import jax
import jax.numpy as jnp
from jax import lax
from jax.experimental import pallas as pl
from jax.experimental.pallas import tpu as pltpu
from jax.sharding import PartitionSpec as P

HD = 64
FREQ = 256
PAIR = 2 * HD
GROUP = 2
BASE, CTRL = 0, 1
F32 = jnp.float32
BF16 = jnp.bfloat16
MESH = pl.DeviceIdType.MESH


def attend_pair(q, k, v, count, near):
    rows = q.shape[0]
    C = rows // count
    total = k.shape[0]
    low = lax.broadcasted_iota(jnp.int32, (rows, PAIR), 1) < HD
    zero = jnp.zeros_like(q)
    both = jnp.concatenate([jnp.where(low, q, zero), jnp.where(low, zero, q)], axis=0)
    scores = lax.dot_general(both, k, (((1,), (1,)), ((), ())), preferred_element_type=F32)
    lane = lax.broadcasted_iota(jnp.int32, (C, 128), 1)
    weights = []
    for h in range(2):
        for b in range(count):
            r0 = (count * h + b) * C
            first, last = b * C, (b + near) * C
            t0, t1 = first // 128, -(-last // 128)
            tiles = []
            for t in range(t0, t1):
                at, end = t * 128, min(t * 128 + 128, total)
                tile = scores[r0 : r0 + C, at:end]
                if at < first:
                    tile = jnp.where(lane[:, : end - at] >= first - at, tile, -1e30)
                if end > last:
                    tile = jnp.where(lane[:, : end - at] < last - at, tile, -1e30)
                tiles.append(tile)
            row = jnp.concatenate(tiles, axis=1)
            top = jnp.max(row, axis=1, keepdims=True)
            expo = [jnp.exp2(row - top).astype(BF16)]
            if t0:
                expo = [jnp.zeros((C, t0 * 128), BF16)] + expo
            if t1 * 128 < total:
                expo = expo + [jnp.zeros((C, total - t1 * 128), BF16)]
            weights.append(jnp.concatenate(expo, axis=1) if len(expo) > 1 else expo[0])
    weights = jnp.concatenate(weights, axis=0)
    ones = jnp.concatenate([v, jnp.ones_like(v)], axis=1)
    mixed = jnp.dot(weights, ones, preferred_element_type=F32)
    mixed = mixed[:, :PAIR] / mixed[:, PAIR:]
    return jnp.where(low, mixed[:rows], mixed[rows:]).astype(BF16)


def kernel(
    dims,
    x_hbm,
    step_ref,
    num_ref,
    den_ref,
    level_ref,
    freq_ref,
    table_ref,
    tw_hbm,
    bq_hbm,
    bk_hbm,
    bv_hbm,
    bo_hbm,
    cq_hbm,
    ck_hbm,
    cv_hbm,
    co_hbm,
    zl_hbm,
    out_ref,
    xg,
    tw,
    wqkv,
    wo,
    mod,
    ms,
    q,
    kv,
    att,
    att_in,
    x_in,
    csum,
    part,
    parts_in,
    give,
    take,
    swap_out,
    swap_in,
    load_sem,
    g_send,
    g_recv,
    h_send,
    h_recv,
    a_send,
    a_recv,
    i_send,
    i_recv,
    p_send,
    p_recv,
    f_send,
    f_recv,
    x_send,
    x_recv,
):
    frames, rows, cols, feat, n_lon, n_head = dims
    C = frames * rows
    T = C * cols
    width = feat * n_head
    groups = cols // GROUP
    G = GROUP * C
    lon, head, cfg = lax.axis_index("lon"), lax.axis_index("head"), lax.axis_index("cfg")
    is_cond = cfg == 0
    lp, lm = lax.rem(lon + 1, n_lon), lax.rem(lon + n_lon - 1, n_lon)
    to_lp, to_lm = (lp, head, cfg), (lm, head, cfg)
    half_feat = feat // 2
    core = lax.rem(lon, 2)
    make = [jnp.where(core == 0, g, groups - 1 - g) for g in range(groups)]
    order = [jnp.where(core == 0, groups - 1 - g, g) for g in range(groups)]
    make_cols = [jnp.where(core == 0, c, cols - 1 - c) for c in range(cols)]
    heads = [head] + [lax.rem(head + k, n_head) for k in range(1, n_head)]
    peers = range(1, n_head)
    to_cfg = (lon, head, 1 - cfg)

    own_copy = pltpu.make_async_copy(x_hbm, xg.at[head], load_sem.at[0])
    own_copy.start()
    loads = [
        (tw_hbm, tw),
        (cq_hbm, wqkv.at[CTRL, :, pl.ds(0, feat)]),
        (ck_hbm, wqkv.at[CTRL, :, pl.ds(feat, feat)]),
        (cv_hbm, wqkv.at[CTRL, :, pl.ds(2 * feat, feat)]),
        (bq_hbm, wqkv.at[BASE, :, pl.ds(0, feat)]),
        (bk_hbm, wqkv.at[BASE, :, pl.ds(feat, feat)]),
        (bv_hbm, wqkv.at[BASE, :, pl.ds(2 * feat, feat)]),
    ]
    for at, w in ((CTRL, co_hbm), (BASE, bo_hbm), (2, zl_hbm)):
        loads += [(w.at[:, pl.ds(d * feat, feat)], wo.at[at, d]) for d in range(n_head)]
    loads = [pltpu.make_async_copy(s, d, load_sem.at[i + 1]) for i, (s, d) in enumerate(loads)]

    barrier = pltpu.get_barrier_semaphore()
    partners = [(lon, heads[k], cfg) for k in peers] + [to_cfg, to_lp, to_lm]
    for who in partners:
        pl.semaphore_signal(barrier, inc=1, device_id=who, device_id_type=MESH)
    for copy in loads:
        copy.start()
    pl.semaphore_wait(barrier, len(partners))

    def send(src, dst, ssem, rsem, who):
        return pltpu.make_async_remote_copy(
            src_ref=src, dst_ref=dst, send_sem=ssem, recv_sem=rsem, device_id=who, device_id_type=MESH
        )

    def to_peer(src, dst, ssem, rsem, k):
        return send(src, dst, ssem, rsem, (lon, heads[k], cfg))

    def gather(c, k):
        return to_peer(x_hbm.at[:, c], xg.at[head, :, c], g_send.at[k, c], g_recv.at[k, c], k)

    def gathered(c, k, slot):
        return to_peer(x_hbm.at[:, c], xg.at[heads[slot], :, c], g_send.at[k, c], g_recv.at[k, c], 1)

    def relay(c, k):
        place = xg.at[heads[4 - k], :, c]
        return to_peer(place, place, g_send.at[2, c], g_recv.at[2, c], k)

    def own_sends(i):
        gather(make_cols[i], 1).start()
        gather(make_cols[i], 3).start()

    def serve(i):
        gathered(make_cols[i], 1, 3).wait_recv()
        gathered(make_cols[i], 3, 1).wait_recv()
        relay(make_cols[i], 1 if i % 2 == 0 else 3).start()
        if i + 3 < cols:
            own_sends(i + 3)

    def own_rows(g):
        return pl.ds(pl.multiple_of(T + g * G, G), G)

    def halo(branch, g, side):
        dst = pl.ds(pl.multiple_of((0 if side == 0 else 2 * T) + g * G, G), G)
        who = to_lp if side == 0 else to_lm
        return send(
            kv.at[branch, own_rows(g)], kv.at[branch, dst], h_send.at[branch, g, side], h_recv.at[branch, g, side], who
        )

    def wait_halo(branch, g, side):
        dst = pl.ds(pl.multiple_of(2 * T * side + g * G, G), G)
        send(
            kv.at[branch, own_rows(g)], kv.at[branch, dst], h_send.at[branch, g, side], h_recv.at[branch, g, side], to_lp
        ).wait_recv()

    def normalise(branch, c, at):
        parts = [xg[j, :, c].reshape(C, feat).astype(F32) for j in range(n_head)]
        if branch == CTRL:
            levels = lax.broadcasted_iota(jnp.int32, (table_ref.shape[0], rows), 0)
            hot = [jnp.where(levels == level_ref[c, f : f + 1, :], 1.0, 0.0).astype(BF16) for f in range(frames)]
            for j in range(n_head):
                table = table_ref[:, j * feat : (j + 1) * feat]
                emb = [
                    lax.dot_general(h, table, (((0,), (0,)), ((), ())), preferred_element_type=F32) for h in hot
                ]
                parts[j] = parts[j] + jnp.concatenate(emb, axis=0)
        center = sum(jnp.sum(u, axis=1, keepdims=True) for u in parts) * (1.0 / width)
        parts = [u - center for u in parts]
        spread = sum(jnp.sum(u * u, axis=1, keepdims=True) for u in parts) * (1.0 / width)
        scale = lax.rsqrt(spread + 1e-06)
        for j in range(n_head):
            sl = pl.ds(j * feat, feat)
            gain = 1.0 + mod[0:1, sl]
            shift = mod[0:1, pl.ds(width + j * feat, feat)]
            ms[branch, pl.ds(at, C), sl] = (parts[j] * scale * gain + shift).astype(BF16)

    def project(branch, g):
        for c in range(GROUP):
            normalise(branch, g * GROUP + c, c * C)
        normed = ms[branch]
        kv[branch, own_rows(g), :] = jnp.dot(
            normed, wqkv[branch, :, feat:], preferred_element_type=F32
        ).astype(BF16)
        for side in range(2):
            halo(branch, g, side).start()
        query = jnp.dot(normed, wqkv[branch, :, :feat], preferred_element_type=F32)
        q[branch, pl.ds(pl.multiple_of(g * G, G), G), :] = (query * (math.log2(math.e) / math.sqrt(HD))).astype(BF16)

    def my_col(j):
        return j * GROUP + cfg

    def other_col(j):
        return j * GROUP + 1 - cfg

    def col_rows(c):
        return pl.ds(pl.multiple_of(c * C, C), C)

    def share_x(j):
        return send(x_hbm.at[:, other_col(j)], x_in.at[j], i_send.at[j], i_recv.at[j], to_cfg)

    def share(branch, j):
        src = att.at[branch, col_rows(other_col(j))]
        return send(src, att_in.at[branch, j], a_send.at[branch, j], a_recv.at[branch, j], to_cfg)

    for i in range(3):
        own_sends(i)
    for j in range(groups):
        share_x(j).start()

    angles = freq_ref[...] * step_ref[0].astype(F32)
    temb = jnp.concatenate([jnp.cos(angles), jnp.sin(angles)], axis=1).astype(BF16)
    loads[0].wait()
    mod[...] = jnp.dot(temb, tw[...], preferred_element_type=F32)
    ones = jnp.ones((8, feat), F32)
    ratio = (ones * num_ref[0].astype(F32)) / (ones * den_ref[0].astype(F32))
    ratio = ratio[0:1, :]
    factor = jnp.where(is_cond, ratio, 1.0 - ratio)
    own_copy.wait()
    for copy in loads[1:]:
        copy.wait()

    for i, g in enumerate(make):
        until = min(cols, (i + 2) * GROUP)
        for n in range(0 if i == 0 else min(cols, (i + 1) * GROUP), until):
            serve(n)
        for c in make_cols[i * GROUP : (i + 1) * GROUP]:
            gathered(c, 2, 2).wait_recv()

        @pl.when(is_cond)
        def _():
            project(CTRL, g)

        project(BASE, g)

    def ctrl_sum(j, k):
        return to_peer(part.at[j, k], parts_in.at[j, n_head - k], p_send.at[j, k], p_recv.at[j, n_head - k], k)

    def ctrl_in(j, k):
        return to_peer(part.at[j, k], parts_in.at[j, k], p_send.at[j, k], p_recv.at[j, k], k)

    def collect(j):
        total = part[j, 0].astype(F32)
        for k in peers:
            ctrl_in(j, k).wait_recv()
            total = total + parts_in[j, k].astype(F32)
        csum[j] = total.astype(BF16)

    def base_sum(j, k):
        return to_peer(give.at[j, k], take.at[j, n_head - k], f_send.at[j, k], f_recv.at[j, n_head - k], k)

    def base_in(j, k):
        return to_peer(give.at[j, k], take.at[j, k], f_send.at[j, k], f_recv.at[j, k], k)

    def swap(j):
        return send(swap_out.at[j], swap_in.at[j], x_send.at[j], x_recv.at[j], to_cfg)

    def ctrl_out(j, done):
        for k in (2, 1, 3, 0):
            part[j, k] = jnp.dot(done, wo[CTRL, heads[k]], preferred_element_type=F32).astype(BF16)
            if k:
                ctrl_sum(j, k).start()

    def final_out(j):
        own = att[BASE, col_rows(my_col(j)), :].astype(F32)
        mixed = (own * factor + att_in[BASE, j].astype(F32) * (1.0 - factor)).astype(BF16)
        for k in (2, 1, 3, 0):
            d = heads[k]
            val = jnp.dot(csum[j], wo[2, d], preferred_element_type=F32) * ratio
            val += jnp.dot(mixed, wo[BASE, d], preferred_element_type=F32)
            give[j, k] = val.astype(BF16)
            if k:
                base_sum(j, k).start()

    def reduce(j):
        c = my_col(j)
        total = xg[head, :, c].reshape(C, feat).astype(F32) * factor
        total = total + x_in[j].reshape(C, feat).astype(F32) * (1.0 - factor)
        total = total + give[j, 0].astype(F32)
        for k in peers:
            base_in(j, k).wait_recv()
            total = total + take[j, k].astype(F32)
        low, high = total[:, :half_feat], total[:, half_feat:]
        other = jnp.where(is_cond, high, low).astype(BF16)
        swap_out[j] = jnp.concatenate([other[: C // 2], other[C // 2 :]], axis=1)
        swap(j).start()
        out_ref[:, c] = jnp.where(is_cond, low, high).astype(BF16).reshape(frames, rows, half_feat)

    def finish(j):
        swap(j).wait_recv()
        other = swap_in[j]
        other = jnp.concatenate([other[:, :half_feat], other[:, half_feat:]], axis=0)
        out_ref[:, other_col(j)] = other.reshape(frames, rows, half_feat)

    near = 2 * cols + 1
    n_keys = (near + GROUP - 1) * C

    def attend(branch, j):
        r0 = pl.multiple_of(j * G, G)
        for p in range(feat // PAIR):
            sl = pl.ds(p * PAIR, PAIR)
            att[branch, pl.ds(r0, G), sl] = attend_pair(
                q[branch, pl.ds(r0, G), sl],
                kv[branch, pl.ds(r0, n_keys), sl],
                kv[branch, pl.ds(r0, n_keys), pl.ds(feat + p * PAIR, PAIR)],
                GROUP,
                near,
            )
        share(branch, j).start()

    first = jnp.where(is_cond, CTRL, BASE)
    for g in range(groups):
        wait_halo(first, g, 1 - core)

    for j in order:
        wait_halo(first, j, core)
        attend(first, j)

        @pl.when(is_cond)
        def _():
            ctrl_out(j, att[CTRL, col_rows(my_col(j)), :])

    @pl.when(jnp.logical_not(is_cond))
    def _():
        for j in order:
            share(CTRL, j).wait_recv()
            ctrl_out(j, att_in[CTRL, j])

    @pl.when(is_cond)
    def _():
        for g in range(groups):
            wait_halo(BASE, g, 1 - core)

    for j in range(groups):
        share_x(j).wait_recv()

    for i, j in enumerate(order):

        @pl.when(is_cond)
        def _():
            wait_halo(BASE, j, core)
            attend(BASE, j)

        collect(j)
        share(BASE, j).wait_recv()
        final_out(j)
        if i >= 2:
            reduce(order[i - 2])

    for j in order[groups - 2 :]:
        reduce(j)

    for j in order:
        finish(j)

    for c in range(cols):
        gather(c, 1).wait_send()
        gather(c, 3).wait_send()
        relay(c, 1).wait_send()

    for g in range(groups):
        for side in range(2):
            halo(BASE, g, side).wait_send()

    @pl.when(is_cond)
    def _():
        for g in range(groups):
            for side in range(2):
                halo(CTRL, g, side).wait_send()
            share(CTRL, g).wait_send()

    for j in range(groups):
        share_x(j).wait_send()
        share(BASE, j).wait_send()
        for k in peers:
            ctrl_sum(j, k).wait_send()
            base_sum(j, k).wait_send()
        swap(j).wait_send()


def local(
    latents,
    timestep,
    guide_num,
    guide_den,
    depth_level,
    depth_table,
    time_weight,
    base_q,
    base_k,
    base_v,
    base_o,
    ctrl_q,
    ctrl_k,
    ctrl_v,
    ctrl_o,
    zero_linear,
):
    x = latents[0].transpose(0, 2, 1, 3)
    frames, cols, rows, feat = x.shape
    n_lon, n_head = lax.axis_size("lon"), lax.axis_size("head")
    C, T, width = frames * rows, frames * rows * cols, feat * n_head
    freqs = jnp.exp(-math.log(10000.0) * jnp.arange(FREQ // 2).astype(F32) / (FREQ // 2))
    freqs = jnp.broadcast_to(freqs[None, :], (16, FREQ // 2))
    dma = pltpu.SemaphoreType.DMA
    vmem = pl.BlockSpec(memory_space=pltpu.VMEM)
    smem = pl.BlockSpec(memory_space=pltpu.SMEM)
    hbm = pl.BlockSpec(memory_space=pl.ANY)
    groups = cols // GROUP
    out = pl.pallas_call(
        functools.partial(kernel, (frames, rows, cols, feat, n_lon, n_head)),
        out_shape=jax.ShapeDtypeStruct((frames, cols, rows, feat // 2), BF16),
        in_specs=[hbm, smem, smem, smem, vmem, vmem, vmem] + [hbm] * 10,
        out_specs=vmem,
        scratch_shapes=[
            pltpu.VMEM((n_head, frames, cols, rows, feat), BF16),
            pltpu.VMEM((FREQ, 2 * width), BF16),
            pltpu.VMEM((2, width, 3 * feat), BF16),
            pltpu.VMEM((3, n_head, feat, feat), BF16),
            pltpu.VMEM((16, 2 * width), F32),
            pltpu.VMEM((2, GROUP * C, width), BF16),
            pltpu.VMEM((2, T, feat), BF16),
            pltpu.VMEM((2, 3 * T, 2 * feat), BF16),
            pltpu.VMEM((2, T, feat), BF16),
            pltpu.VMEM((2, groups, C, feat), BF16),
            pltpu.VMEM((groups, frames, rows, feat), BF16),
            pltpu.VMEM((groups, C, feat), BF16),
            pltpu.VMEM((groups, n_head, C, feat), BF16),
            pltpu.VMEM((groups, n_head, C, feat), BF16),
            pltpu.VMEM((groups, n_head, C, feat), BF16),
            pltpu.VMEM((groups, n_head, C, feat), BF16),
            pltpu.VMEM((groups, C // 2, feat), BF16),
            pltpu.VMEM((groups, C // 2, feat), BF16),
            dma((20,)),
            dma((n_head, cols)),
            dma((n_head, cols)),
            dma((2, groups, 2)),
            dma((2, groups, 2)),
            dma((2, groups)),
            dma((2, groups)),
            dma((groups,)),
            dma((groups,)),
            dma((groups, n_head)),
            dma((groups, n_head)),
            dma((groups, n_head)),
            dma((groups, n_head)),
            dma((groups,)),
            dma((groups,)),
        ],
        compiler_params=pltpu.CompilerParams(
            collective_id=0, has_side_effects=True, vmem_limit_bytes=58 * 1024 * 1024
        ),
    )(
        x,
        timestep,
        guide_num,
        guide_den,
        depth_level.transpose(2, 0, 1),
        freqs,
        depth_table,
        time_weight,
        base_q,
        base_k,
        base_v,
        base_o,
        ctrl_q,
        ctrl_k,
        ctrl_v,
        ctrl_o,
        zero_linear,
    )
    return out.transpose(0, 2, 1, 3)


def solution(mesh):
    return jax.shard_map(
        local,
        mesh=mesh,
        in_specs=(
            P("cfg", None, None, "lon", "head"),
            P(),
            P(),
            P(),
            P(None, None, "lon"),
            P(),
            P(),
            P(None, "head"),
            P(None, "head"),
            P(None, "head"),
            P("head", None),
            P(None, "head"),
            P(None, "head"),
            P(None, "head"),
            P("head", None),
            P("head", None),
        ),
        out_specs=P(None, None, "lon", ("head", "cfg")),
        check_vma=False,
    )
```

```python
import functools
import math

import jax
import jax.numpy as jnp
import numpy as np
from jax import lax
from jax.experimental import pallas as pl
from jax.experimental.pallas import tpu as pltpu
from jax.sharding import PartitionSpec as P

HD = 64
FREQ = 256
PAIR = 2 * HD
GROUP = 2
BASE, CTRL = 0, 1
F32 = jnp.float32
BF16 = jnp.bfloat16
MESH = pl.DeviceIdType.MESH


def attend_pair(q, k, v, count, near):
    rows = q.shape[0]
    C = rows // count
    total = k.shape[0]
    low = lax.broadcasted_iota(jnp.int32, (rows, PAIR), 1) < HD
    zero = jnp.zeros_like(q)
    both = jnp.concatenate([jnp.where(low, q, zero), jnp.where(low, zero, q)], axis=0)
    scores = lax.dot_general(both, k, (((1,), (1,)), ((), ())), preferred_element_type=F32)
    lane = lax.broadcasted_iota(jnp.int32, (C, 128), 1)
    weights = []
    for h in range(2):
        for b in range(count):
            r0 = (count * h + b) * C
            first, last = b * C, (b + near) * C
            t0, t1 = first // 128, -(-last // 128)
            tiles = []
            for t in range(t0, t1):
                at, end = t * 128, min(t * 128 + 128, total)
                tile = scores[r0 : r0 + C, at:end]
                if at < first:
                    tile = jnp.where(lane[:, : end - at] >= first - at, tile, -1e30)
                if end > last:
                    tile = jnp.where(lane[:, : end - at] < last - at, tile, -1e30)
                tiles.append(tile)
            row = jnp.concatenate(tiles, axis=1)
            top = jnp.max(row, axis=1, keepdims=True)
            expo = [jnp.exp2(row - top).astype(BF16)]
            if t0:
                expo = [jnp.zeros((C, t0 * 128), BF16)] + expo
            if t1 * 128 < total:
                expo = expo + [jnp.zeros((C, total - t1 * 128), BF16)]
            weights.append(jnp.concatenate(expo, axis=1) if len(expo) > 1 else expo[0])
    weights = jnp.concatenate(weights, axis=0)
    ones = jnp.concatenate([v, jnp.ones_like(v)], axis=1)
    mixed = jnp.dot(weights, ones, preferred_element_type=F32)
    mixed = mixed[:, :PAIR] / mixed[:, PAIR:]
    return jnp.where(low, mixed[:rows], mixed[rows:]).astype(BF16)


def kernel(
    dims,
    x_hbm,
    step_ref,
    num_ref,
    den_ref,
    level_ref,
    freq_ref,
    table_ref,
    tw_hbm,
    bq_hbm,
    bk_hbm,
    bv_hbm,
    bo_hbm,
    cq_hbm,
    ck_hbm,
    cv_hbm,
    co_hbm,
    zl_hbm,
    out_ref,
    xg,
    tw,
    wqkv,
    wo,
    mod,
    ms,
    q,
    kv,
    att,
    att_in,
    x_in,
    csum,
    part,
    parts_in,
    give,
    take,
    swap_out,
    swap_in,
    load_sem,
    g_send,
    g_recv,
    h_send,
    h_recv,
    a_send,
    a_recv,
    i_send,
    i_recv,
    p_send,
    p_recv,
    f_send,
    f_recv,
    x_send,
    x_recv,
):
    frames, rows, cols, feat, n_lon, n_head = dims
    C = frames * rows
    T = C * cols
    width = feat * n_head
    groups = cols // GROUP
    G = GROUP * C
    lon, head, cfg = lax.axis_index("lon"), lax.axis_index("head"), lax.axis_index("cfg")
    is_cond = cfg == 0
    lp, lm = lax.rem(lon + 1, n_lon), lax.rem(lon + n_lon - 1, n_lon)
    to_lp, to_lm = (lp, head, cfg), (lm, head, cfg)
    half_feat = feat // 2
    core = lax.rem(lon, 2)
    make = [jnp.where(core == 0, g, groups - 1 - g) for g in range(groups)]
    order = [jnp.where(core == 0, groups - 1 - g, g) for g in range(groups)]
    make_cols = [jnp.where(core == 0, c, cols - 1 - c) for c in range(cols)]
    heads = [head] + [lax.rem(head + k, n_head) for k in range(1, n_head)]
    peers = range(1, n_head)
    to_cfg = (lon, head, 1 - cfg)

    own_copy = pltpu.make_async_copy(x_hbm, xg.at[head], load_sem.at[0])
    own_copy.start()
    loads = [
        (tw_hbm, tw),
        (cq_hbm, wqkv.at[CTRL, :, pl.ds(0, feat)]),
        (ck_hbm, wqkv.at[CTRL, :, pl.ds(feat, feat)]),
        (cv_hbm, wqkv.at[CTRL, :, pl.ds(2 * feat, feat)]),
        (bq_hbm, wqkv.at[BASE, :, pl.ds(0, feat)]),
        (bk_hbm, wqkv.at[BASE, :, pl.ds(feat, feat)]),
        (bv_hbm, wqkv.at[BASE, :, pl.ds(2 * feat, feat)]),
    ]
    for at, w in ((CTRL, co_hbm), (BASE, bo_hbm), (2, zl_hbm)):
        loads += [(w.at[:, pl.ds(d * feat, feat)], wo.at[at, d]) for d in range(n_head)]
    loads = [pltpu.make_async_copy(s, d, load_sem.at[i + 1]) for i, (s, d) in enumerate(loads)]

    barrier = pltpu.get_barrier_semaphore()
    partners = [(lon, heads[k], cfg) for k in peers] + [to_cfg, to_lp, to_lm]
    for who in partners:
        pl.semaphore_signal(barrier, inc=1, device_id=who, device_id_type=MESH)
    for copy in loads:
        copy.start()
    pl.semaphore_wait(barrier, len(partners))

    def send(src, dst, ssem, rsem, who):
        return pltpu.make_async_remote_copy(
            src_ref=src, dst_ref=dst, send_sem=ssem, recv_sem=rsem, device_id=who, device_id_type=MESH
        )

    def to_peer(src, dst, ssem, rsem, k):
        return send(src, dst, ssem, rsem, (lon, heads[k], cfg))

    def gather(c, k):
        return to_peer(x_hbm.at[:, c], xg.at[head, :, c], g_send.at[k, c], g_recv.at[k, c], k)

    def gathered(c, k, slot):
        return to_peer(x_hbm.at[:, c], xg.at[heads[slot], :, c], g_send.at[k, c], g_recv.at[k, c], 1)

    def relay(c, k):
        place = xg.at[heads[4 - k], :, c]
        return to_peer(place, place, g_send.at[2, c], g_recv.at[2, c], k)

    def own_sends(i):
        gather(make_cols[i], 1).start()
        gather(make_cols[i], 3).start()

    def serve(i):
        gathered(make_cols[i], 1, 3).wait_recv()
        gathered(make_cols[i], 3, 1).wait_recv()
        relay(make_cols[i], 1 if i % 2 == 0 else 3).start()
        if i + 3 < cols:
            own_sends(i + 3)

    def own_rows(g):
        return pl.ds(pl.multiple_of(T + g * G, G), G)

    def halo(branch, g, side):
        dst = pl.ds(pl.multiple_of((0 if side == 0 else 2 * T) + g * G, G), G)
        who = to_lp if side == 0 else to_lm
        return send(
            kv.at[branch, own_rows(g)], kv.at[branch, dst], h_send.at[branch, g, side], h_recv.at[branch, g, side], who
        )

    def wait_halo(branch, g, side):
        dst = pl.ds(pl.multiple_of(2 * T * side + g * G, G), G)
        send(
            kv.at[branch, own_rows(g)], kv.at[branch, dst], h_send.at[branch, g, side], h_recv.at[branch, g, side], to_lp
        ).wait_recv()

    def normalise(branch, c, at):
        parts = [xg[j, :, c].reshape(C, feat).astype(F32) for j in range(n_head)]
        if branch == CTRL:
            levels = lax.broadcasted_iota(jnp.int32, (table_ref.shape[0], rows), 0)
            hot = [jnp.where(levels == level_ref[c, f : f + 1, :], 1.0, 0.0).astype(BF16) for f in range(frames)]
            for j in range(n_head):
                table = table_ref[:, j * feat : (j + 1) * feat]
                emb = [
                    lax.dot_general(h, table, (((0,), (0,)), ((), ())), preferred_element_type=F32) for h in hot
                ]
                parts[j] = parts[j] + jnp.concatenate(emb, axis=0)
        center = sum(jnp.sum(u, axis=1, keepdims=True) for u in parts) * (1.0 / width)
        parts = [u - center for u in parts]
        spread = sum(jnp.sum(u * u, axis=1, keepdims=True) for u in parts) * (1.0 / width)
        scale = lax.rsqrt(spread + 1e-06)
        for j in range(n_head):
            sl = pl.ds(j * feat, feat)
            gain = 1.0 + mod[0:1, sl]
            shift = mod[0:1, pl.ds(width + j * feat, feat)]
            ms[branch, pl.ds(at, C), sl] = (parts[j] * scale * gain + shift).astype(BF16)

    def project(branch, g):
        for c in range(GROUP):
            normalise(branch, g * GROUP + c, c * C)
        normed = ms[branch]
        kv[branch, own_rows(g), :] = jnp.dot(
            normed, wqkv[branch, :, feat:], preferred_element_type=F32
        ).astype(BF16)
        for side in range(2):
            halo(branch, g, side).start()
        query = jnp.dot(normed, wqkv[branch, :, :feat], preferred_element_type=F32)
        q[branch, pl.ds(pl.multiple_of(g * G, G), G), :] = (query * (math.log2(math.e) / math.sqrt(HD))).astype(BF16)

    order_cols = [jnp.where(core == 0, cols - 1 - p, p) for p in range(cols)]
    cond_cols = [order_cols[p] for p in (2, 4, 5)]
    uncond_cols = [order_cols[p] for p in (0, 1, 3)]

    def my_col(n):
        return jnp.where(is_cond, cond_cols[n], uncond_cols[n])

    def other_col(n):
        return jnp.where(is_cond, uncond_cols[n], cond_cols[n])

    def col_rows(c):
        return pl.ds(pl.multiple_of(c * C, C), C)

    def share_x(j):
        return send(x_hbm.at[:, other_col(j)], x_in.at[j], i_send.at[j], i_recv.at[j], to_cfg)

    def share(branch, j):
        src = att.at[branch, col_rows(other_col(j))]
        return send(src, att_in.at[branch, j], a_send.at[branch, j], a_recv.at[branch, j], to_cfg)

    for i in range(3):
        own_sends(i)
    for j in range(groups):
        share_x(j).start()

    angles = jnp.broadcast_to(freq_ref[...], (16, FREQ // 2)) * step_ref[0].astype(F32)
    temb = jnp.concatenate([jnp.cos(angles), jnp.sin(angles)], axis=1).astype(BF16)
    loads[0].wait()
    mod[...] = jnp.dot(temb, tw[...], preferred_element_type=F32)
    ones = jnp.ones((8, feat), F32)
    ratio = (ones * num_ref[0].astype(F32)) / (ones * den_ref[0].astype(F32))
    ratio = ratio[0:1, :]
    factor = jnp.where(is_cond, ratio, 1.0 - ratio)
    own_copy.wait()
    for copy in loads[1:]:
        copy.wait()

    for i, g in enumerate(make):
        until = min(cols, (i + 2) * GROUP)
        for n in range(0 if i == 0 else min(cols, (i + 1) * GROUP), until):
            serve(n)
        for c in make_cols[i * GROUP : (i + 1) * GROUP]:
            gathered(c, 2, 2).wait_recv()

        @pl.when(is_cond)
        def _():
            project(CTRL, g)

        project(BASE, g)

    def ctrl_sum(j, k):
        return to_peer(part.at[j, k], parts_in.at[j, n_head - k], p_send.at[j, k], p_recv.at[j, n_head - k], k)

    def ctrl_in(j, k):
        return to_peer(part.at[j, k], parts_in.at[j, k], p_send.at[j, k], p_recv.at[j, k], k)

    def collect(j):
        total = part[j, 0].astype(F32)
        for k in peers:
            ctrl_in(j, k).wait_recv()
            total = total + parts_in[j, k].astype(F32)
        csum[j] = total.astype(BF16)

    def base_sum(j, k):
        return to_peer(give.at[j, k], take.at[j, n_head - k], f_send.at[j, k], f_recv.at[j, n_head - k], k)

    def base_in(j, k):
        return to_peer(give.at[j, k], take.at[j, k], f_send.at[j, k], f_recv.at[j, k], k)

    def swap(j):
        return send(swap_out.at[j], swap_in.at[j], x_send.at[j], x_recv.at[j], to_cfg)

    def ctrl_out(j, done):
        for k in (2, 1, 3, 0):
            part[j, k] = jnp.dot(done, wo[CTRL, heads[k]], preferred_element_type=F32).astype(BF16)
            if k:
                ctrl_sum(j, k).start()

    def final_out(j):
        own = att[BASE, col_rows(my_col(j)), :].astype(F32)
        mixed = (own * factor + att_in[BASE, j].astype(F32) * (1.0 - factor)).astype(BF16)
        for k in (2, 1, 3, 0):
            d = heads[k]
            val = jnp.dot(csum[j], wo[2, d], preferred_element_type=F32) * ratio
            val += jnp.dot(mixed, wo[BASE, d], preferred_element_type=F32)
            give[j, k] = val.astype(BF16)
            if k:
                base_sum(j, k).start()

    def reduce(j):
        c = my_col(j)
        total = xg[head, :, c].reshape(C, feat).astype(F32) * factor
        total = total + x_in[j].reshape(C, feat).astype(F32) * (1.0 - factor)
        total = total + give[j, 0].astype(F32)
        for k in peers:
            base_in(j, k).wait_recv()
            total = total + take[j, k].astype(F32)
        low, high = total[:, :half_feat], total[:, half_feat:]
        other = jnp.where(is_cond, high, low).astype(BF16)
        swap_out[j] = jnp.concatenate([other[: C // 2], other[C // 2 :]], axis=1)
        swap(j).start()
        out_ref[:, c] = jnp.where(is_cond, low, high).astype(BF16).reshape(frames, rows, half_feat)

    def finish(j):
        swap(j).wait_recv()
        other = swap_in[j]
        other = jnp.concatenate([other[:, :half_feat], other[:, half_feat:]], axis=0)
        out_ref[:, other_col(j)] = other.reshape(frames, rows, half_feat)

    near = 2 * cols + 1

    def attend(branch, c, count):
        here = pl.ds(pl.multiple_of(c * C, C), count * C)
        keys = pl.ds(pl.multiple_of(c * C, C), (near + count - 1) * C)
        for p in range(feat // PAIR):
            sl = pl.ds(p * PAIR, PAIR)
            att[branch, here, sl] = attend_pair(
                q[branch, here, sl],
                kv[branch, keys, sl],
                kv[branch, keys, pl.ds(feat + p * PAIR, PAIR)],
                count,
                near,
            )

    first = jnp.where(is_cond, CTRL, BASE)
    for g in range(groups):
        wait_halo(first, g, 1 - core)

    for i, j in enumerate(order):
        wait_halo(first, j, core)
        attend(first, j * GROUP, GROUP)

        @pl.when(is_cond)
        def _():
            for n in ((0, 1), (2,), ())[i]:
                share(CTRL, n).start()
            for n in ((), (0,), (1, 2))[i]:
                ctrl_out(n, att[CTRL, col_rows(my_col(n)), :])

        @pl.when(jnp.logical_not(is_cond))
        def _():
            for n in ((), (0,), (1, 2))[i]:
                share(BASE, n).start()

    for n in range(groups):
        share_x(n).wait_recv()

    def complete(n):
        collect(n)
        share(BASE, n).wait_recv()
        final_out(n)

    @pl.when(jnp.logical_not(is_cond))
    def _():
        for n in range(groups):
            share(CTRL, n).wait_recv()
            ctrl_out(n, att_in[CTRL, n])
        for n in range(groups):
            complete(n)

    @pl.when(is_cond)
    def _():
        for g in range(groups):
            wait_halo(BASE, g, 1 - core)
        wait_halo(BASE, order[0], core)
        attend(BASE, order[0] * GROUP, GROUP)
        share(BASE, 0).start()
        share(BASE, 1).start()
        wait_halo(BASE, order[1], core)
        attend(BASE, order[1] * GROUP, GROUP)
        share(BASE, 2).start()
        complete(0)
        wait_halo(BASE, order[2], core)
        attend(BASE, order_cols[4], 1)
        complete(1)
        attend(BASE, order_cols[5], 1)
        complete(2)

    for n in range(groups):
        reduce(n)

    for n in range(groups):
        finish(n)

    for c in range(cols):
        gather(c, 1).wait_send()
        gather(c, 3).wait_send()
        relay(c, 1).wait_send()

    for g in range(groups):
        for side in range(2):
            halo(BASE, g, side).wait_send()

    @pl.when(is_cond)
    def _():
        for g in range(groups):
            for side in range(2):
                halo(CTRL, g, side).wait_send()
            share(CTRL, g).wait_send()

    for j in range(groups):
        share_x(j).wait_send()
        share(BASE, j).wait_send()
        for k in peers:
            ctrl_sum(j, k).wait_send()
            base_sum(j, k).wait_send()
        swap(j).wait_send()


def local(
    latents,
    timestep,
    guide_num,
    guide_den,
    depth_level,
    depth_table,
    time_weight,
    base_q,
    base_k,
    base_v,
    base_o,
    ctrl_q,
    ctrl_k,
    ctrl_v,
    ctrl_o,
    zero_linear,
):
    x = latents[0].transpose(0, 2, 1, 3)
    frames, cols, rows, feat = x.shape
    n_lon, n_head = lax.axis_size("lon"), lax.axis_size("head")
    C, T, width = frames * rows, frames * rows * cols, feat * n_head
    freqs = np.exp(-math.log(10000.0) * np.arange(FREQ // 2) / (FREQ // 2)).astype(np.float32)
    freqs = jnp.asarray(freqs[None, :])
    dma = pltpu.SemaphoreType.DMA
    vmem = pl.BlockSpec(memory_space=pltpu.VMEM)
    smem = pl.BlockSpec(memory_space=pltpu.SMEM)
    hbm = pl.BlockSpec(memory_space=pl.ANY)
    groups = cols // GROUP
    out = pl.pallas_call(
        functools.partial(kernel, (frames, rows, cols, feat, n_lon, n_head)),
        out_shape=jax.ShapeDtypeStruct((frames, cols, rows, feat // 2), BF16),
        in_specs=[hbm, smem, smem, smem, vmem, vmem, vmem] + [hbm] * 10,
        out_specs=vmem,
        scratch_shapes=[
            pltpu.VMEM((n_head, frames, cols, rows, feat), BF16),
            pltpu.VMEM((FREQ, 2 * width), BF16),
            pltpu.VMEM((2, width, 3 * feat), BF16),
            pltpu.VMEM((3, n_head, feat, feat), BF16),
            pltpu.VMEM((16, 2 * width), F32),
            pltpu.VMEM((2, GROUP * C, width), BF16),
            pltpu.VMEM((2, T, feat), BF16),
            pltpu.VMEM((2, 3 * T, 2 * feat), BF16),
            pltpu.VMEM((2, T, feat), BF16),
            pltpu.VMEM((2, groups, C, feat), BF16),
            pltpu.VMEM((groups, frames, rows, feat), BF16),
            pltpu.VMEM((groups, C, feat), BF16),
            pltpu.VMEM((groups, n_head, C, feat), BF16),
            pltpu.VMEM((groups, n_head, C, feat), BF16),
            pltpu.VMEM((groups, n_head, C, feat), BF16),
            pltpu.VMEM((groups, n_head, C, feat), BF16),
            pltpu.VMEM((groups, C // 2, feat), BF16),
            pltpu.VMEM((groups, C // 2, feat), BF16),
            dma((20,)),
            dma((n_head, cols)),
            dma((n_head, cols)),
            dma((2, groups, 2)),
            dma((2, groups, 2)),
            dma((2, groups)),
            dma((2, groups)),
            dma((groups,)),
            dma((groups,)),
            dma((groups, n_head)),
            dma((groups, n_head)),
            dma((groups, n_head)),
            dma((groups, n_head)),
            dma((groups,)),
            dma((groups,)),
        ],
        compiler_params=pltpu.CompilerParams(
            collective_id=0, has_side_effects=True, vmem_limit_bytes=58 * 1024 * 1024
        ),
    )(
        x,
        timestep,
        guide_num,
        guide_den,
        depth_level.transpose(2, 0, 1),
        freqs,
        depth_table,
        time_weight,
        base_q,
        base_k,
        base_v,
        base_o,
        ctrl_q,
        ctrl_k,
        ctrl_v,
        ctrl_o,
        zero_linear,
    )
    return out.transpose(0, 2, 1, 3)


def solution(mesh):
    return jax.shard_map(
        local,
        mesh=mesh,
        in_specs=(
            P("cfg", None, None, "lon", "head"),
            P(),
            P(),
            P(),
            P(None, None, "lon"),
            P(),
            P(),
            P(None, "head"),
            P(None, "head"),
            P(None, "head"),
            P("head", None),
            P(None, "head"),
            P(None, "head"),
            P(None, "head"),
            P("head", None),
            P("head", None),
        ),
        out_specs=P(None, None, "lon", ("head", "cfg")),
        check_vma=False,
    )
```

```python
import functools
import math

import jax
import jax.numpy as jnp
import numpy as np
from jax import lax
from jax.experimental import pallas as pl
from jax.experimental.pallas import tpu as pltpu
from jax.sharding import PartitionSpec as P

HD = 64
FREQ = 256
PAIR = 2 * HD
GROUP = 2
BASE, CTRL = 0, 1
F32 = jnp.float32
BF16 = jnp.bfloat16
MESH = pl.DeviceIdType.MESH


def attend_pair(q, k, v, count, near):
    rows = q.shape[0]
    C = rows // count
    total = k.shape[0]
    low = lax.broadcasted_iota(jnp.int32, (rows, PAIR), 1) < HD
    zero = jnp.zeros_like(q)
    both = jnp.concatenate([jnp.where(low, q, zero), jnp.where(low, zero, q)], axis=0)
    scores = lax.dot_general(both, k, (((1,), (1,)), ((), ())), preferred_element_type=F32)
    lane = lax.broadcasted_iota(jnp.int32, (C, 128), 1)
    weights = []
    for h in range(2):
        for b in range(count):
            r0 = (count * h + b) * C
            first, last = b * C, (b + near) * C
            t0, t1 = first // 128, -(-last // 128)
            tiles = []
            for t in range(t0, t1):
                at, end = t * 128, min(t * 128 + 128, total)
                tile = scores[r0 : r0 + C, at:end]
                if at < first:
                    tile = jnp.where(lane[:, : end - at] >= first - at, tile, -1e30)
                if end > last:
                    tile = jnp.where(lane[:, : end - at] < last - at, tile, -1e30)
                tiles.append(tile)
            row = jnp.concatenate(tiles, axis=1)
            top = jnp.max(row, axis=1, keepdims=True)
            expo = [jnp.exp2(row - top).astype(BF16)]
            if t0:
                expo = [jnp.zeros((C, t0 * 128), BF16)] + expo
            if t1 * 128 < total:
                expo = expo + [jnp.zeros((C, total - t1 * 128), BF16)]
            weights.append(jnp.concatenate(expo, axis=1) if len(expo) > 1 else expo[0])
    weights = jnp.concatenate(weights, axis=0)
    ones = jnp.concatenate([v, jnp.ones_like(v)], axis=1)
    mixed = jnp.dot(weights, ones, preferred_element_type=F32)
    mixed = mixed[:, :PAIR] / mixed[:, PAIR:]
    return jnp.where(low, mixed[:rows], mixed[rows:]).astype(BF16)


def kernel(
    dims,
    x_hbm,
    step_ref,
    num_ref,
    den_ref,
    level_ref,
    freq_ref,
    table_ref,
    tw_hbm,
    bq_hbm,
    bk_hbm,
    bv_hbm,
    bo_hbm,
    cq_hbm,
    ck_hbm,
    cv_hbm,
    co_hbm,
    zl_hbm,
    out_ref,
    xg,
    tw,
    wqkv,
    wo,
    mod,
    ms,
    q,
    kv,
    att,
    att_in,
    x_in,
    csum,
    part,
    parts_in,
    give,
    take,
    swap_out,
    swap_in,
    load_sem,
    g_send,
    g_recv,
    h_send,
    h_recv,
    a_send,
    a_recv,
    i_send,
    i_recv,
    p_send,
    p_recv,
    f_send,
    f_recv,
    x_send,
    x_recv,
):
    frames, rows, cols, feat, n_lon, n_head = dims
    C = frames * rows
    T = C * cols
    width = feat * n_head
    groups = cols // GROUP
    G = GROUP * C
    lon, head, cfg = lax.axis_index("lon"), lax.axis_index("head"), lax.axis_index("cfg")
    is_cond = cfg == 0
    lp, lm = lax.rem(lon + 1, n_lon), lax.rem(lon + n_lon - 1, n_lon)
    to_lp, to_lm = (lp, head, cfg), (lm, head, cfg)
    half_feat = feat // 2
    core = lax.rem(lon, 2)
    make = [jnp.where(core == 0, g, groups - 1 - g) for g in range(groups)]
    order = [jnp.where(core == 0, groups - 1 - g, g) for g in range(groups)]
    make_cols = [jnp.where(core == 0, c, cols - 1 - c) for c in range(cols)]
    heads = [head] + [lax.rem(head + k, n_head) for k in range(1, n_head)]
    peers = range(1, n_head)
    to_cfg = (lon, head, 1 - cfg)

    own_copy = pltpu.make_async_copy(x_hbm, xg.at[head], load_sem.at[0])
    own_copy.start()
    loads = [
        (tw_hbm, tw),
        (cq_hbm, wqkv.at[CTRL, :, pl.ds(0, feat)]),
        (ck_hbm, wqkv.at[CTRL, :, pl.ds(feat, feat)]),
        (cv_hbm, wqkv.at[CTRL, :, pl.ds(2 * feat, feat)]),
        (bq_hbm, wqkv.at[BASE, :, pl.ds(0, feat)]),
        (bk_hbm, wqkv.at[BASE, :, pl.ds(feat, feat)]),
        (bv_hbm, wqkv.at[BASE, :, pl.ds(2 * feat, feat)]),
    ]
    for at, w in ((CTRL, co_hbm), (BASE, bo_hbm), (2, zl_hbm)):
        loads += [(w.at[:, pl.ds(d * feat, feat)], wo.at[at, d]) for d in range(n_head)]
    loads = [pltpu.make_async_copy(s, d, load_sem.at[i + 1]) for i, (s, d) in enumerate(loads)]

    barrier = pltpu.get_barrier_semaphore()
    partners = [(lon, heads[k], cfg) for k in peers] + [to_cfg, to_lp, to_lm]
    for who in partners:
        pl.semaphore_signal(barrier, inc=1, device_id=who, device_id_type=MESH)
    for copy in loads:
        copy.start()
    pl.semaphore_wait(barrier, len(partners))

    def send(src, dst, ssem, rsem, who):
        return pltpu.make_async_remote_copy(
            src_ref=src, dst_ref=dst, send_sem=ssem, recv_sem=rsem, device_id=who, device_id_type=MESH
        )

    def to_peer(src, dst, ssem, rsem, k):
        return send(src, dst, ssem, rsem, (lon, heads[k], cfg))

    def gather(c, k):
        return to_peer(x_hbm.at[:, c], xg.at[head, :, c], g_send.at[k, c], g_recv.at[k, c], k)

    def gathered(c, k, slot):
        return to_peer(x_hbm.at[:, c], xg.at[heads[slot], :, c], g_send.at[k, c], g_recv.at[k, c], 1)

    def relay(c, k):
        place = xg.at[heads[4 - k], :, c]
        return to_peer(place, place, g_send.at[2, c], g_recv.at[2, c], k)

    def own_sends(i):
        gather(make_cols[i], 1).start()
        gather(make_cols[i], 3).start()

    def serve(i):
        gathered(make_cols[i], 1, 3).wait_recv()
        gathered(make_cols[i], 3, 1).wait_recv()
        relay(make_cols[i], 1 if i % 2 == 0 else 3).start()
        if i + 4 < cols:
            own_sends(i + 4)

    def own_rows(g):
        return pl.ds(pl.multiple_of(T + g * G, G), G)

    def halo(branch, g, side):
        dst = pl.ds(pl.multiple_of((0 if side == 0 else 2 * T) + g * G, G), G)
        who = to_lp if side == 0 else to_lm
        return send(
            kv.at[branch, own_rows(g)], kv.at[branch, dst], h_send.at[branch, g, side], h_recv.at[branch, g, side], who
        )

    def send_halo(branch, g):
        for side in range(2):
            halo(branch, g, side).start()

    def wait_halo(branch, g, side):
        dst = pl.ds(pl.multiple_of(2 * T * side + g * G, G), G)
        send(
            kv.at[branch, own_rows(g)], kv.at[branch, dst], h_send.at[branch, g, side], h_recv.at[branch, g, side], to_lp
        ).wait_recv()

    def normalise(branch, c, at):
        parts = [xg[j, :, c].reshape(C, feat).astype(F32) for j in range(n_head)]
        if branch == CTRL:
            levels = lax.broadcasted_iota(jnp.int32, (table_ref.shape[0], rows), 0)
            hot = [jnp.where(levels == level_ref[c, f : f + 1, :], 1.0, 0.0).astype(BF16) for f in range(frames)]
            for j in range(n_head):
                table = table_ref[:, j * feat : (j + 1) * feat]
                emb = [
                    lax.dot_general(h, table, (((0,), (0,)), ((), ())), preferred_element_type=F32) for h in hot
                ]
                parts[j] = parts[j] + jnp.concatenate(emb, axis=0)
        center = sum(jnp.sum(u, axis=1, keepdims=True) for u in parts) * (1.0 / width)
        parts = [u - center for u in parts]
        spread = sum(jnp.sum(u * u, axis=1, keepdims=True) for u in parts) * (1.0 / width)
        scale = lax.rsqrt(spread + 1e-06)
        for j in range(n_head):
            sl = pl.ds(j * feat, feat)
            gain = 1.0 + mod[0:1, sl]
            shift = mod[0:1, pl.ds(width + j * feat, feat)]
            ms[branch, pl.ds(at, C), sl] = (parts[j] * scale * gain + shift).astype(BF16)

    def project(branch, g):
        for c in range(GROUP):
            normalise(branch, g * GROUP + c, c * C)
        normed = ms[branch]
        kv[branch, own_rows(g), :] = jnp.dot(
            normed, wqkv[branch, :, feat:], preferred_element_type=F32
        ).astype(BF16)
        if branch == CTRL:
            send_halo(branch, g)
        else:

            @pl.when(jnp.logical_not(is_cond))
            def _():
                send_halo(branch, g)

        query = jnp.dot(normed, wqkv[branch, :, :feat], preferred_element_type=F32)
        q[branch, pl.ds(pl.multiple_of(g * G, G), G), :] = (query * (math.log2(math.e) / math.sqrt(HD))).astype(BF16)

    order_cols = [jnp.where(core == 0, cols - 1 - p, p) for p in range(cols)]
    cond_cols = [order_cols[p] for p in (2, 4, 5)]
    uncond_cols = [order_cols[p] for p in (0, 1, 3)]

    def my_col(n):
        return jnp.where(is_cond, cond_cols[n], uncond_cols[n])

    def other_col(n):
        return jnp.where(is_cond, uncond_cols[n], cond_cols[n])

    def col_rows(c):
        return pl.ds(pl.multiple_of(c * C, C), C)

    def share_x(j):
        return send(x_hbm.at[:, other_col(j)], x_in.at[j], i_send.at[j], i_recv.at[j], to_cfg)

    def share(branch, j):
        src = att.at[branch, col_rows(other_col(j))]
        return send(src, att_in.at[branch, j], a_send.at[branch, j], a_recv.at[branch, j], to_cfg)

    for i in range(4):
        own_sends(i)
    for j in range(groups):
        share_x(j).start()

    angles = jnp.broadcast_to(freq_ref[...], (16, FREQ // 2)) * step_ref[0].astype(F32)
    temb = jnp.concatenate([jnp.cos(angles), jnp.sin(angles)], axis=1).astype(BF16)
    loads[0].wait()
    mod[...] = jnp.dot(temb, tw[...], preferred_element_type=F32)
    ones = jnp.ones((8, feat), F32)
    ratio = (ones * num_ref[0].astype(F32)) / (ones * den_ref[0].astype(F32))
    ratio = ratio[0:1, :]
    factor = jnp.where(is_cond, ratio, 1.0 - ratio)

    for i, g in enumerate(make):
        until = min(cols, (i + 2) * GROUP)
        for n in range(0 if i == 0 else min(cols, (i + 1) * GROUP), until):
            serve(n)
        if i == 0:
            own_copy.wait()
            for copy in loads[1:]:
                copy.wait()
        for c in make_cols[i * GROUP : (i + 1) * GROUP]:
            gathered(c, 2, 2).wait_recv()

        @pl.when(is_cond)
        def _():
            project(CTRL, g)

        project(BASE, g)

    @pl.when(is_cond)
    def _():
        for g in make:
            send_halo(BASE, g)

    def ctrl_sum(j, k):
        return to_peer(part.at[j, k], parts_in.at[j, n_head - k], p_send.at[j, k], p_recv.at[j, n_head - k], k)

    def ctrl_in(j, k):
        return to_peer(part.at[j, k], parts_in.at[j, k], p_send.at[j, k], p_recv.at[j, k], k)

    def collect(j):
        total = part[j, 0].astype(F32)
        for k in peers:
            ctrl_in(j, k).wait_recv()
            total = total + parts_in[j, k].astype(F32)
        csum[j] = total.astype(BF16)

    def base_sum(j, k):
        return to_peer(give.at[j, k], take.at[j, n_head - k], f_send.at[j, k], f_recv.at[j, n_head - k], k)

    def base_in(j, k):
        return to_peer(give.at[j, k], take.at[j, k], f_send.at[j, k], f_recv.at[j, k], k)

    def swap(j):
        return send(swap_out.at[j], swap_in.at[j], x_send.at[j], x_recv.at[j], to_cfg)

    def ctrl_out(j, done):
        for k in (2, 1, 3, 0):
            part[j, k] = jnp.dot(done, wo[CTRL, heads[k]], preferred_element_type=F32).astype(BF16)
            if k:
                ctrl_sum(j, k).start()

    def final_out(j):
        own = att[BASE, col_rows(my_col(j)), :].astype(F32)
        mixed = (own * factor + att_in[BASE, j].astype(F32) * (1.0 - factor)).astype(BF16)
        for k in (2, 1, 3, 0):
            d = heads[k]
            val = jnp.dot(csum[j], wo[2, d], preferred_element_type=F32) * ratio
            val += jnp.dot(mixed, wo[BASE, d], preferred_element_type=F32)
            give[j, k] = val.astype(BF16)
            if k:
                base_sum(j, k).start()

    def reduce(j):
        c = my_col(j)
        total = xg[head, :, c].reshape(C, feat).astype(F32) * factor
        total = total + x_in[j].reshape(C, feat).astype(F32) * (1.0 - factor)
        total = total + give[j, 0].astype(F32)
        for k in peers:
            base_in(j, k).wait_recv()
            total = total + take[j, k].astype(F32)
        low, high = total[:, :half_feat], total[:, half_feat:]
        other = jnp.where(is_cond, high, low).astype(BF16)
        swap_out[j] = jnp.concatenate([other[: C // 2], other[C // 2 :]], axis=1)
        swap(j).start()
        out_ref[:, c] = jnp.where(is_cond, low, high).reshape(frames, rows, half_feat)

    def finish(j):
        swap(j).wait_recv()
        other = swap_in[j]
        other = jnp.concatenate([other[:, :half_feat], other[:, half_feat:]], axis=0)
        out_ref[:, other_col(j)] = other.astype(F32).reshape(frames, rows, half_feat)

    near = 2 * cols + 1

    def attend(branch, c, count):
        here = pl.ds(pl.multiple_of(c * C, C), count * C)
        keys = pl.ds(pl.multiple_of(c * C, C), (near + count - 1) * C)
        for p in range(feat // PAIR):
            sl = pl.ds(p * PAIR, PAIR)
            att[branch, here, sl] = attend_pair(
                q[branch, here, sl],
                kv[branch, keys, sl],
                kv[branch, keys, pl.ds(feat + p * PAIR, PAIR)],
                count,
                near,
            )

    first = jnp.where(is_cond, CTRL, BASE)
    for g in range(groups):
        wait_halo(first, g, 1 - core)

    for i, j in enumerate(order):
        wait_halo(first, j, core)
        attend(first, j * GROUP, GROUP)

        @pl.when(is_cond)
        def _():
            for n in ((0, 1), (2,), ())[i]:
                share(CTRL, n).start()
            for n in ((), (0,), (1, 2))[i]:
                ctrl_out(n, att[CTRL, col_rows(my_col(n)), :])

        @pl.when(jnp.logical_not(is_cond))
        def _():
            for n in ((), (0,), (1, 2))[i]:
                share(BASE, n).start()

    for n in range(groups):
        share_x(n).wait_recv()

    def complete(n):
        collect(n)
        share(BASE, n).wait_recv()
        final_out(n)

    @pl.when(jnp.logical_not(is_cond))
    def _():
        for n in range(groups):
            share(CTRL, n).wait_recv()
            ctrl_out(n, att_in[CTRL, n])
        for n in range(groups):
            complete(n)

    @pl.when(is_cond)
    def _():
        for g in range(groups):
            wait_halo(BASE, g, 1 - core)
        wait_halo(BASE, order[0], core)
        attend(BASE, order[0] * GROUP, GROUP)
        share(BASE, 0).start()
        share(BASE, 1).start()
        wait_halo(BASE, order[1], core)
        attend(BASE, order[1] * GROUP, GROUP)
        share(BASE, 2).start()
        complete(0)
        wait_halo(BASE, order[2], core)
        attend(BASE, order_cols[4], 1)
        complete(1)
        attend(BASE, order_cols[5], 1)
        complete(2)

    for n in range(groups):
        reduce(n)

    for n in range(groups):
        finish(n)

    for c in range(cols):
        gather(c, 1).wait_send()
        gather(c, 3).wait_send()
        relay(c, 1).wait_send()

    for g in range(groups):
        for side in range(2):
            halo(BASE, g, side).wait_send()

    @pl.when(is_cond)
    def _():
        for g in range(groups):
            for side in range(2):
                halo(CTRL, g, side).wait_send()
            share(CTRL, g).wait_send()

    for j in range(groups):
        share_x(j).wait_send()
        share(BASE, j).wait_send()
        for k in peers:
            ctrl_sum(j, k).wait_send()
            base_sum(j, k).wait_send()
        swap(j).wait_send()


def local(
    latents,
    timestep,
    guide_num,
    guide_den,
    depth_level,
    depth_table,
    time_weight,
    base_q,
    base_k,
    base_v,
    base_o,
    ctrl_q,
    ctrl_k,
    ctrl_v,
    ctrl_o,
    zero_linear,
):
    x = latents[0].transpose(0, 2, 1, 3)
    frames, cols, rows, feat = x.shape
    n_lon, n_head = lax.axis_size("lon"), lax.axis_size("head")
    C, T, width = frames * rows, frames * rows * cols, feat * n_head
    freqs = np.exp(-math.log(10000.0) * np.arange(FREQ // 2) / (FREQ // 2)).astype(np.float32)
    freqs = jnp.asarray(freqs[None, :])
    dma = pltpu.SemaphoreType.DMA
    vmem = pl.BlockSpec(memory_space=pltpu.VMEM)
    smem = pl.BlockSpec(memory_space=pltpu.SMEM)
    hbm = pl.BlockSpec(memory_space=pl.ANY)
    groups = cols // GROUP
    out = pl.pallas_call(
        functools.partial(kernel, (frames, rows, cols, feat, n_lon, n_head)),
        out_shape=jax.ShapeDtypeStruct((frames, cols, rows, feat // 2), F32),
        in_specs=[hbm, smem, smem, smem, vmem, vmem, vmem] + [hbm] * 10,
        out_specs=vmem,
        scratch_shapes=[
            pltpu.VMEM((n_head, frames, cols, rows, feat), BF16),
            pltpu.VMEM((FREQ, 2 * width), BF16),
            pltpu.VMEM((2, width, 3 * feat), BF16),
            pltpu.VMEM((3, n_head, feat, feat), BF16),
            pltpu.VMEM((16, 2 * width), F32),
            pltpu.VMEM((2, GROUP * C, width), BF16),
            pltpu.VMEM((2, T, feat), BF16),
            pltpu.VMEM((2, 3 * T, 2 * feat), BF16),
            pltpu.VMEM((2, T, feat), BF16),
            pltpu.VMEM((2, groups, C, feat), BF16),
            pltpu.VMEM((groups, frames, rows, feat), BF16),
            pltpu.VMEM((groups, C, feat), BF16),
            pltpu.VMEM((groups, n_head, C, feat), BF16),
            pltpu.VMEM((groups, n_head, C, feat), BF16),
            pltpu.VMEM((groups, n_head, C, feat), BF16),
            pltpu.VMEM((groups, n_head, C, feat), BF16),
            pltpu.VMEM((groups, C // 2, feat), BF16),
            pltpu.VMEM((groups, C // 2, feat), BF16),
            dma((20,)),
            dma((n_head, cols)),
            dma((n_head, cols)),
            dma((2, groups, 2)),
            dma((2, groups, 2)),
            dma((2, groups)),
            dma((2, groups)),
            dma((groups,)),
            dma((groups,)),
            dma((groups, n_head)),
            dma((groups, n_head)),
            dma((groups, n_head)),
            dma((groups, n_head)),
            dma((groups,)),
            dma((groups,)),
        ],
        compiler_params=pltpu.CompilerParams(
            collective_id=0, has_side_effects=True, vmem_limit_bytes=58 * 1024 * 1024
        ),
    )(
        x,
        timestep,
        guide_num,
        guide_den,
        depth_level.transpose(2, 0, 1),
        freqs,
        depth_table,
        time_weight,
        base_q,
        base_k,
        base_v,
        base_o,
        ctrl_q,
        ctrl_k,
        ctrl_v,
        ctrl_o,
        zero_linear,
    )
    return out.transpose(0, 2, 1, 3).astype(BF16)


def solution(mesh):
    return jax.shard_map(
        local,
        mesh=mesh,
        in_specs=(
            P("cfg", None, None, "lon", "head"),
            P(),
            P(),
            P(),
            P(None, None, "lon"),
            P(),
            P(),
            P(None, "head"),
            P(None, "head"),
            P(None, "head"),
            P("head", None),
            P(None, "head"),
            P(None, "head"),
            P(None, "head"),
            P("head", None),
            P("head", None),
        ),
        out_specs=P(None, None, "lon", ("head", "cfg")),
        check_vma=False,
    )
```

```python
import functools
import math

import jax
import jax.numpy as jnp
import numpy as np
from jax import lax
from jax.experimental import pallas as pl
from jax.experimental.pallas import tpu as pltpu
from jax.sharding import PartitionSpec as P

HD = 64
FREQ = 256
PAIR = 2 * HD
GROUP = 2
BASE, CTRL = 0, 1
F32 = jnp.float32
BF16 = jnp.bfloat16
MESH = pl.DeviceIdType.MESH


def attend_pair(q, k, v, count, near):
    rows = q.shape[0]
    C = rows // count
    total = k.shape[0]
    low = lax.broadcasted_iota(jnp.int32, (rows, PAIR), 1) < HD
    zero = jnp.zeros_like(q)
    both = jnp.concatenate([jnp.where(low, q, zero), jnp.where(low, zero, q)], axis=0)
    scores = lax.dot_general(both, k, (((1,), (1,)), ((), ())), preferred_element_type=F32)
    lane = lax.broadcasted_iota(jnp.int32, (C, 128), 1)
    weights = []
    for h in range(2):
        for b in range(count):
            r0 = (count * h + b) * C
            first, last = b * C, (b + near) * C
            t0, t1 = first // 128, -(-last // 128)
            tiles = []
            for t in range(t0, t1):
                at, end = t * 128, min(t * 128 + 128, total)
                tile = scores[r0 : r0 + C, at:end]
                if at < first:
                    tile = jnp.where(lane[:, : end - at] >= first - at, tile, -1e30)
                if end > last:
                    tile = jnp.where(lane[:, : end - at] < last - at, tile, -1e30)
                tiles.append(tile)
            row = jnp.concatenate(tiles, axis=1)
            top = jnp.max(row, axis=1, keepdims=True)
            expo = [jnp.exp2(row - top).astype(BF16)]
            if t0:
                expo = [jnp.zeros((C, t0 * 128), BF16)] + expo
            if t1 * 128 < total:
                expo = expo + [jnp.zeros((C, total - t1 * 128), BF16)]
            weights.append(jnp.concatenate(expo, axis=1) if len(expo) > 1 else expo[0])
    weights = jnp.concatenate(weights, axis=0)
    ones = jnp.concatenate([v, jnp.ones_like(v)], axis=1)
    mixed = jnp.dot(weights, ones, preferred_element_type=F32)
    mixed = mixed[:, :PAIR] / mixed[:, PAIR:]
    return jnp.where(low, mixed[:rows], mixed[rows:]).astype(BF16)


def kernel(
    dims,
    x_hbm,
    step_ref,
    num_ref,
    den_ref,
    level_ref,
    freq_ref,
    table_ref,
    tw_hbm,
    bq_hbm,
    bk_hbm,
    bv_hbm,
    bo_hbm,
    cq_hbm,
    ck_hbm,
    cv_hbm,
    co_hbm,
    zl_hbm,
    out_ref,
    xg,
    tw,
    wqkv,
    wo,
    mod,
    ms,
    q,
    kv,
    att,
    att_in,
    x_in,
    csum,
    part,
    parts_in,
    give,
    take,
    swap_out,
    swap_in,
    load_sem,
    g_send,
    g_recv,
    h_send,
    h_recv,
    a_send,
    a_recv,
    i_send,
    i_recv,
    p_send,
    p_recv,
    f_send,
    f_recv,
    x_send,
    x_recv,
):
    frames, rows, cols, feat, n_lon, n_head = dims
    C = frames * rows
    T = C * cols
    width = feat * n_head
    groups = cols // GROUP
    G = GROUP * C
    lon, head, cfg = lax.axis_index("lon"), lax.axis_index("head"), lax.axis_index("cfg")
    is_cond = cfg == 0
    lp, lm = lax.rem(lon + 1, n_lon), lax.rem(lon + n_lon - 1, n_lon)
    to_lp, to_lm = (lp, head, cfg), (lm, head, cfg)
    half_feat = feat // 2
    core = lax.rem(lon, 2)
    make = [jnp.where(core == 0, g, groups - 1 - g) for g in range(groups)]
    order = [jnp.where(core == 0, groups - 1 - g, g) for g in range(groups)]
    make_cols = [jnp.where(core == 0, c, cols - 1 - c) for c in range(cols)]
    heads = [head] + [lax.rem(head + k, n_head) for k in range(1, n_head)]
    peers = range(1, n_head)
    to_cfg = (lon, head, 1 - cfg)

    own_copy = pltpu.make_async_copy(x_hbm, xg.at[head], load_sem.at[0])
    own_copy.start()
    loads = [
        (tw_hbm, tw),
        (cq_hbm, wqkv.at[CTRL, :, pl.ds(0, feat)]),
        (ck_hbm, wqkv.at[CTRL, :, pl.ds(feat, feat)]),
        (cv_hbm, wqkv.at[CTRL, :, pl.ds(2 * feat, feat)]),
        (bq_hbm, wqkv.at[BASE, :, pl.ds(0, feat)]),
        (bk_hbm, wqkv.at[BASE, :, pl.ds(feat, feat)]),
        (bv_hbm, wqkv.at[BASE, :, pl.ds(2 * feat, feat)]),
    ]
    for at, w in ((CTRL, co_hbm), (BASE, bo_hbm), (2, zl_hbm)):
        loads += [(w.at[:, pl.ds(d * feat, feat)], wo.at[at, d]) for d in range(n_head)]
    loads = [pltpu.make_async_copy(s, d, load_sem.at[i + 1]) for i, (s, d) in enumerate(loads)]

    barrier = pltpu.get_barrier_semaphore()
    partners = [(lon, heads[k], cfg) for k in peers] + [to_cfg, to_lp, to_lm]
    for who in partners:
        pl.semaphore_signal(barrier, inc=1, device_id=who, device_id_type=MESH)
    for copy in loads:
        copy.start()
    pl.semaphore_wait(barrier, len(partners))

    def send(src, dst, ssem, rsem, who):
        return pltpu.make_async_remote_copy(
            src_ref=src, dst_ref=dst, send_sem=ssem, recv_sem=rsem, device_id=who, device_id_type=MESH
        )

    def to_peer(src, dst, ssem, rsem, k):
        return send(src, dst, ssem, rsem, (lon, heads[k], cfg))

    def gather(c, k):
        return to_peer(x_hbm.at[:, c], xg.at[head, :, c], g_send.at[k, c], g_recv.at[k, c], k)

    def gathered(c, k, slot):
        return to_peer(x_hbm.at[:, c], xg.at[heads[slot], :, c], g_send.at[k, c], g_recv.at[k, c], 1)

    def relay(c, k):
        place = xg.at[heads[4 - k], :, c]
        return to_peer(place, place, g_send.at[2, c], g_recv.at[2, c], k)

    def own_sends(i):
        gather(make_cols[i], 1).start()
        gather(make_cols[i], 3).start()

    def serve(i):
        gathered(make_cols[i], 1, 3).wait_recv()
        gathered(make_cols[i], 3, 1).wait_recv()
        relay(make_cols[i], 1 if i % 2 == 0 else 3).start()
        if i + 4 < cols:
            own_sends(i + 4)

    def own_rows(g):
        return pl.ds(pl.multiple_of(T + g * G, G), G)

    def halo(branch, g, side):
        dst = pl.ds(pl.multiple_of((0 if side == 0 else 2 * T) + g * G, G), G)
        who = to_lp if side == 0 else to_lm
        return send(
            kv.at[branch, own_rows(g)], kv.at[branch, dst], h_send.at[branch, g, side], h_recv.at[branch, g, side], who
        )

    def send_halo(branch, g):
        for side in range(2):
            halo(branch, g, side).start()

    def wait_halo(branch, g, side):
        dst = pl.ds(pl.multiple_of(2 * T * side + g * G, G), G)
        send(
            kv.at[branch, own_rows(g)], kv.at[branch, dst], h_send.at[branch, g, side], h_recv.at[branch, g, side], to_lp
        ).wait_recv()

    def normalise(branch, c, at):
        parts = [xg[j, :, c].reshape(C, feat).astype(F32) for j in range(n_head)]
        if branch == CTRL:
            levels = lax.broadcasted_iota(jnp.int32, (table_ref.shape[0], rows), 0)
            hot = [jnp.where(levels == level_ref[c, f : f + 1, :], 1.0, 0.0).astype(BF16) for f in range(frames)]
            for j in range(n_head):
                table = table_ref[:, j * feat : (j + 1) * feat]
                emb = [
                    lax.dot_general(h, table, (((0,), (0,)), ((), ())), preferred_element_type=F32) for h in hot
                ]
                parts[j] = parts[j] + jnp.concatenate(emb, axis=0)
        center = sum(jnp.sum(u, axis=1, keepdims=True) for u in parts) * (1.0 / width)
        parts = [u - center for u in parts]
        spread = sum(jnp.sum(u * u, axis=1, keepdims=True) for u in parts) * (1.0 / width)
        scale = lax.rsqrt(spread + 1e-06)
        for j in range(n_head):
            sl = pl.ds(j * feat, feat)
            gain = 1.0 + mod[0:1, sl]
            shift = mod[0:1, pl.ds(width + j * feat, feat)]
            ms[branch, pl.ds(at, C), sl] = (parts[j] * scale * gain + shift).astype(BF16)

    def project(branch, g):
        for c in range(GROUP):
            normalise(branch, g * GROUP + c, c * C)
        normed = ms[branch]
        kv[branch, own_rows(g), :] = jnp.dot(
            normed, wqkv[branch, :, feat:], preferred_element_type=F32
        ).astype(BF16)
        if branch == CTRL:
            send_halo(branch, g)
        else:

            @pl.when(jnp.logical_not(is_cond))
            def _():
                send_halo(branch, g)

        query = jnp.dot(normed, wqkv[branch, :, :feat], preferred_element_type=F32)
        q[branch, pl.ds(pl.multiple_of(g * G, G), G), :] = (query * (math.log2(math.e) / math.sqrt(HD))).astype(BF16)

    order_cols = [jnp.where(core == 0, cols - 1 - p, p) for p in range(cols)]
    cond_cols = [order_cols[p] for p in (2, 4, 5)]
    uncond_cols = [order_cols[p] for p in (0, 1, 3)]

    def my_col(n):
        return jnp.where(is_cond, cond_cols[n], uncond_cols[n])

    def other_col(n):
        return jnp.where(is_cond, uncond_cols[n], cond_cols[n])

    def col_rows(c):
        return pl.ds(pl.multiple_of(c * C, C), C)

    def share_x(j):
        return send(x_hbm.at[:, other_col(j)], x_in.at[j], i_send.at[j], i_recv.at[j], to_cfg)

    def share(branch, j):
        src = att.at[branch, col_rows(other_col(j))]
        return send(src, att_in.at[branch, j], a_send.at[branch, j], a_recv.at[branch, j], to_cfg)

    for i in range(4):
        own_sends(i)
    for j in range(groups):
        share_x(j).start()

    angles = jnp.broadcast_to(freq_ref[...], (16, FREQ // 2)) * step_ref[0].astype(F32)
    temb = jnp.concatenate([jnp.cos(angles), jnp.sin(angles)], axis=1).astype(BF16)
    loads[0].wait()
    mod[...] = jnp.dot(temb, tw[...], preferred_element_type=F32)
    ones = jnp.ones((8, feat), F32)
    ratio = (ones * num_ref[0].astype(F32)) / (ones * den_ref[0].astype(F32))
    ratio = ratio[0:1, :]
    factor = jnp.where(is_cond, ratio, 1.0 - ratio)

    for i, g in enumerate(make):
        until = min(cols, (i + 2) * GROUP)
        for n in range(0 if i == 0 else min(cols, (i + 1) * GROUP), until):
            serve(n)
        if i == 0:
            own_copy.wait()
            for copy in loads[1:]:
                copy.wait()
        for c in make_cols[i * GROUP : (i + 1) * GROUP]:
            gathered(c, 2, 2).wait_recv()

        @pl.when(is_cond)
        def _():
            project(CTRL, g)
            if i >= 1:
                send_halo(BASE, make[i - 1])

        project(BASE, g)

    @pl.when(is_cond)
    def _():
        send_halo(BASE, make[groups - 1])

    def ctrl_sum(j, k):
        return to_peer(part.at[j, k], parts_in.at[j, n_head - k], p_send.at[j, k], p_recv.at[j, n_head - k], k)

    def ctrl_in(j, k):
        return to_peer(part.at[j, k], parts_in.at[j, k], p_send.at[j, k], p_recv.at[j, k], k)

    def collect(j):
        total = part[j, 0].astype(F32)
        for k in peers:
            ctrl_in(j, k).wait_recv()
            total = total + parts_in[j, k].astype(F32)
        csum[j] = total.astype(BF16)

    def base_sum(j, k):
        return to_peer(give.at[j, k], take.at[j, n_head - k], f_send.at[j, k], f_recv.at[j, n_head - k], k)

    def base_in(j, k):
        return to_peer(give.at[j, k], take.at[j, k], f_send.at[j, k], f_recv.at[j, k], k)

    def swap(j):
        return send(swap_out.at[j], swap_in.at[j], x_send.at[j], x_recv.at[j], to_cfg)

    def ctrl_out(j, done):
        for k in (2, 1, 3, 0):
            part[j, k] = jnp.dot(done, wo[CTRL, heads[k]], preferred_element_type=F32).astype(BF16)
            if k:
                ctrl_sum(j, k).start()

    def final_out(j):
        own = att[BASE, col_rows(my_col(j)), :].astype(F32)
        mixed = (own * factor + att_in[BASE, j].astype(F32) * (1.0 - factor)).astype(BF16)
        for k in (2, 1, 3, 0):
            d = heads[k]
            val = jnp.dot(csum[j], wo[2, d], preferred_element_type=F32) * ratio
            val += jnp.dot(mixed, wo[BASE, d], preferred_element_type=F32)
            give[j, k] = val.astype(BF16)
            if k:
                base_sum(j, k).start()

    def reduce(j):
        c = my_col(j)
        total = xg[head, :, c].reshape(C, feat).astype(F32) * factor
        total = total + x_in[j].reshape(C, feat).astype(F32) * (1.0 - factor)
        total = total + give[j, 0].astype(F32)
        for k in peers:
            base_in(j, k).wait_recv()
            total = total + take[j, k].astype(F32)
        low, high = total[:, :half_feat], total[:, half_feat:]
        other = jnp.where(is_cond, high, low).astype(BF16)
        swap_out[j] = jnp.concatenate([other[: C // 2], other[C // 2 :]], axis=1)
        swap(j).start()
        out_ref[:, c] = jnp.where(is_cond, low, high).astype(BF16).reshape(frames, rows, half_feat)

    def finish(j):
        swap(j).wait_recv()
        other = swap_in[j]
        other = jnp.concatenate([other[:, :half_feat], other[:, half_feat:]], axis=0)
        out_ref[:, other_col(j)] = other.reshape(frames, rows, half_feat)

    near = 2 * cols + 1

    def attend(branch, c, count):
        here = pl.ds(pl.multiple_of(c * C, C), count * C)
        keys = pl.ds(pl.multiple_of(c * C, C), (near + count - 1) * C)
        for p in range(feat // PAIR):
            sl = pl.ds(p * PAIR, PAIR)
            att[branch, here, sl] = attend_pair(
                q[branch, here, sl],
                kv[branch, keys, sl],
                kv[branch, keys, pl.ds(feat + p * PAIR, PAIR)],
                count,
                near,
            )

    first = jnp.where(is_cond, CTRL, BASE)
    for g in range(groups):
        wait_halo(first, g, 1 - core)

    for i, j in enumerate(order):
        wait_halo(first, j, core)
        attend(first, j * GROUP, GROUP)

        @pl.when(is_cond)
        def _():
            for n in ((0, 1), (2,), ())[i]:
                share(CTRL, n).start()
            for n in ((), (0,), (1, 2))[i]:
                ctrl_out(n, att[CTRL, col_rows(my_col(n)), :])

        @pl.when(jnp.logical_not(is_cond))
        def _():
            for n in ((), (0,), (1, 2))[i]:
                share(BASE, n).start()

    for n in range(groups):
        share_x(n).wait_recv()

    def complete(n):
        collect(n)
        share(BASE, n).wait_recv()
        final_out(n)

    @pl.when(jnp.logical_not(is_cond))
    def _():
        for n in range(groups):
            share(CTRL, n).wait_recv()
            ctrl_out(n, att_in[CTRL, n])
        for n in range(groups):
            complete(n)

    @pl.when(is_cond)
    def _():
        for g in range(groups):
            wait_halo(BASE, g, 1 - core)
        wait_halo(BASE, order[0], core)
        attend(BASE, order[0] * GROUP, GROUP)
        share(BASE, 0).start()
        share(BASE, 1).start()
        wait_halo(BASE, order[1], core)
        attend(BASE, order[1] * GROUP, GROUP)
        share(BASE, 2).start()
        complete(0)
        wait_halo(BASE, order[2], core)
        attend(BASE, order_cols[4], 1)
        complete(1)
        attend(BASE, order_cols[5], 1)
        complete(2)

    for n in range(groups):
        reduce(n)

    for n in range(groups):
        finish(n)

    for c in range(cols):
        gather(c, 1).wait_send()
        gather(c, 3).wait_send()
        relay(c, 1).wait_send()

    for g in range(groups):
        for side in range(2):
            halo(BASE, g, side).wait_send()

    @pl.when(is_cond)
    def _():
        for g in range(groups):
            for side in range(2):
                halo(CTRL, g, side).wait_send()
            share(CTRL, g).wait_send()

    for j in range(groups):
        share_x(j).wait_send()
        share(BASE, j).wait_send()
        for k in peers:
            ctrl_sum(j, k).wait_send()
            base_sum(j, k).wait_send()
        swap(j).wait_send()


def local(
    latents,
    timestep,
    guide_num,
    guide_den,
    depth_level,
    depth_table,
    time_weight,
    base_q,
    base_k,
    base_v,
    base_o,
    ctrl_q,
    ctrl_k,
    ctrl_v,
    ctrl_o,
    zero_linear,
):
    x = latents[0].transpose(0, 2, 1, 3)
    frames, cols, rows, feat = x.shape
    n_lon, n_head = lax.axis_size("lon"), lax.axis_size("head")
    C, T, width = frames * rows, frames * rows * cols, feat * n_head
    freqs = np.exp(-math.log(10000.0) * np.arange(FREQ // 2) / (FREQ // 2)).astype(np.float32)
    freqs = jnp.asarray(freqs[None, :])
    dma = pltpu.SemaphoreType.DMA
    vmem = pl.BlockSpec(memory_space=pltpu.VMEM)
    smem = pl.BlockSpec(memory_space=pltpu.SMEM)
    hbm = pl.BlockSpec(memory_space=pl.ANY)
    groups = cols // GROUP
    out = pl.pallas_call(
        functools.partial(kernel, (frames, rows, cols, feat, n_lon, n_head)),
        out_shape=jax.ShapeDtypeStruct((frames, cols, rows, feat // 2), BF16),
        in_specs=[hbm, smem, smem, smem, vmem, vmem, vmem] + [hbm] * 10,
        out_specs=vmem,
        scratch_shapes=[
            pltpu.VMEM((n_head, frames, cols, rows, feat), BF16),
            pltpu.VMEM((FREQ, 2 * width), BF16),
            pltpu.VMEM((2, width, 3 * feat), BF16),
            pltpu.VMEM((3, n_head, feat, feat), BF16),
            pltpu.VMEM((16, 2 * width), F32),
            pltpu.VMEM((2, GROUP * C, width), BF16),
            pltpu.VMEM((2, T, feat), BF16),
            pltpu.VMEM((2, 3 * T, 2 * feat), BF16),
            pltpu.VMEM((2, T, feat), BF16),
            pltpu.VMEM((2, groups, C, feat), BF16),
            pltpu.VMEM((groups, frames, rows, feat), BF16),
            pltpu.VMEM((groups, C, feat), BF16),
            pltpu.VMEM((groups, n_head, C, feat), BF16),
            pltpu.VMEM((groups, n_head, C, feat), BF16),
            pltpu.VMEM((groups, n_head, C, feat), BF16),
            pltpu.VMEM((groups, n_head, C, feat), BF16),
            pltpu.VMEM((groups, C // 2, feat), BF16),
            pltpu.VMEM((groups, C // 2, feat), BF16),
            dma((20,)),
            dma((n_head, cols)),
            dma((n_head, cols)),
            dma((2, groups, 2)),
            dma((2, groups, 2)),
            dma((2, groups)),
            dma((2, groups)),
            dma((groups,)),
            dma((groups,)),
            dma((groups, n_head)),
            dma((groups, n_head)),
            dma((groups, n_head)),
            dma((groups, n_head)),
            dma((groups,)),
            dma((groups,)),
        ],
        compiler_params=pltpu.CompilerParams(
            collective_id=0, has_side_effects=True, vmem_limit_bytes=58 * 1024 * 1024
        ),
    )(
        x,
        timestep,
        guide_num,
        guide_den,
        depth_level.transpose(2, 0, 1),
        freqs,
        depth_table,
        time_weight,
        base_q,
        base_k,
        base_v,
        base_o,
        ctrl_q,
        ctrl_k,
        ctrl_v,
        ctrl_o,
        zero_linear,
    )
    return out.transpose(0, 2, 1, 3)


def solution(mesh):
    return jax.shard_map(
        local,
        mesh=mesh,
        in_specs=(
            P("cfg", None, None, "lon", "head"),
            P(),
            P(),
            P(),
            P(None, None, "lon"),
            P(),
            P(),
            P(None, "head"),
            P(None, "head"),
            P(None, "head"),
            P("head", None),
            P(None, "head"),
            P(None, "head"),
            P(None, "head"),
            P("head", None),
            P("head", None),
        ),
        out_specs=P(None, None, "lon", ("head", "cfg")),
        check_vma=False,
    )
```
